32 devices in a mesh: row: 4 (over z), col: 4 (over x, core), depth: 2 (over y).
Axes of the slice: x: 2, y: 2, z: 4, core: 2. Of those that a mesh axis runs over, the one named last changes fastest.
Arguments:
- x_matrix: bfloat16 [576, 576], P(('row', 'depth'), 'col'), may hold values from -0.25 to 0.25
- tangent: bfloat16 [576, 576], P(('row', 'depth'), 'col'), may hold values from -6 to 6
- fill_x: int32 [5, 5], replicated, may hold values from 0 to 1, as said below
- fill_t: int32 [5, 5], replicated, may hold values from 0 to 1, as said below
Outputs:
- tangent_next: float32 [576, 576], P(('row', 'depth'), 'col')
The draws below stay inside these ranges and needn't reach their ends.
Inputs may be any that keep to these rules, and one draw needn't show every extreme that they name: `fill_x`: 1 where the block of X is filled, else 0; every diagonal block is filled. `fill_t`: 1 where the block of X' is filled, else 0; every diagonal block is filled.
All inputs are finite; a program needn't handle non-finite values.
Results may differ from the reference program's by a relative error of at most 0.00098.
Values may be sent and summed in bfloat16 or wider, within the bound.
No kernel may reach another device: no remote copies, remote signals or barrier semaphores. Data moves between devices by JAX's collectives and lax.ppermute only.
A program may use at most 64 MiB of HBM per device.

```python
import jax
import jax.numpy as jnp
from jax import lax

BLOCK = 128
MATRIX = 576


def fill_pattern(key, salt):
    key = jax.random.fold_in(key, salt)
    level_key, pick_key = jax.random.split(key)
    count = (MATRIX + BLOCK - 1) // BLOCK
    levels = jax.random.randint(level_key, (count,), 1, 8)
    picks = jax.random.randint(pick_key, (count, count), 0, 8)
    index = lax.iota(jnp.int32, count)
    diagonal = index[:, None] == index[None, :]
    filled = (picks < levels[:, None]) | diagonal
    return filled.astype(jnp.int32)


def draw_fill_x(key, part):
    return fill_pattern(key, 11)


def draw_fill_t(key, part):
    return fill_pattern(key, 23)


def block_levels(key, shape, pieces, smallest, largest):
    def one(dim, blocks):
        steps = jax.random.uniform(jax.random.fold_in(jax.random.fold_in(key, 6), dim), (blocks,), jnp.float32, smallest / len(pieces), largest / len(pieces))
        return jnp.repeat(jnp.exp(steps), shape[dim] // blocks).reshape((-1,) + (1,) * (len(shape) - dim - 1))

    level = one(*pieces[0])
    for cut in pieces[1:]:
        level = level * one(*cut)
    return level


def scatter_about(key, extent, spread, bound, pieces=(), kind=jnp.bfloat16):
    result = spread * jax.random.normal(key, extent, jnp.float32)
    if pieces:
        result = result * block_levels(key, extent, pieces, -0.22, 0.18)
    return jnp.clip(result, -bound, bound).astype(kind)


def setup_inputs(seed: int = 0) -> dict:
    arg_keys = jax.random.split(jax.random.key(seed), 5)
    x_matrix = scatter_about(arg_keys[0], (MATRIX, MATRIX), MATRIX ** -0.5, 0.25, ((0, 8), (1, 4)))
    tangent = scatter_about(arg_keys[1], (MATRIX, MATRIX), 1.0, 6.0, ((0, 8), (1, 4)))
    fill_x = draw_fill_x(jax.random.fold_in(arg_keys[4], 71), 0)
    fill_t = draw_fill_t(jax.random.fold_in(arg_keys[4], 71), 0)
    return {"x_matrix": x_matrix, "tangent": tangent, "fill_x": fill_x, "fill_t": fill_t}


def expand(fill):
    full = jnp.repeat(jnp.repeat(fill.astype(jnp.float32), BLOCK, axis=0), BLOCK, axis=1)
    return full[:MATRIX, :MATRIX]


def product(left, right):
    return jnp.dot(left, right, preferred_element_type=jnp.float32)


def reference(x_matrix, tangent, fill_x, fill_t):
    masked_x = (x_matrix.astype(jnp.float32) * expand(fill_x)).astype(jnp.bfloat16)
    masked_t = (tangent.astype(jnp.float32) * expand(fill_t)).astype(jnp.bfloat16)
    square = product(masked_x, masked_x).astype(jnp.bfloat16)
    cross = product(masked_t, masked_x).astype(jnp.bfloat16)
    total = product(masked_t, square) + product(masked_x, cross) + product(square, masked_t)
    return 1.5 * masked_t.astype(jnp.float32) - 0.5 * total
```

```python
import functools

import jax
import jax.numpy as jnp
from jax import lax
from jax.experimental import pallas as pl
from jax.experimental.pallas import tpu as pltpu
from jax.sharding import PartitionSpec as P

BLOCK = 128
LANES = 128
VMEM = pl.BlockSpec(memory_space=pltpu.VMEM)
SMEM = pl.BlockSpec(memory_space=pltpu.SMEM)
LIMIT = 48 * 1024 * 1024


def aligned(rows):
    return -(-rows // 16) * 16


def swap(value, axis, offset):
    size = lax.axis_size(axis)
    return lax.ppermute(value, axis, [(i, i ^ offset) for i in range(size)])


def block_fill(fill_ref, row_start, col_start, rows, width):
    count = fill_ref.shape[0]
    row_ids = row_start + lax.broadcasted_iota(jnp.int32, (rows, width), 0)
    col_ids = col_start + lax.broadcasted_iota(jnp.int32, (rows, width), 1)
    first_row, first_col = row_start // BLOCK, col_start // BLOCK
    mask = jnp.zeros((rows, width), jnp.float32)
    for i in range((rows - 2) // BLOCK + 2):
        row_at = first_row + i
        in_row = (row_ids >= row_at * BLOCK) & (row_ids < (row_at + 1) * BLOCK)
        for j in range((width - 2) // BLOCK + 2):
            col_at = first_col + j
            here = in_row & (col_ids >= col_at * BLOCK) & (col_ids < (col_at + 1) * BLOCK)
            flag = fill_ref[jnp.minimum(row_at, count - 1), jnp.minimum(col_at, count - 1)]
            mask = jnp.where(here, flag.astype(jnp.float32), mask)
    return mask


def pack_kernel(x_ref, t_ref, fill_x_ref, fill_t_ref, out_ref):
    rows, width = x_ref.shape
    row_at = lax.axis_index("row") * lax.axis_size("depth") + lax.axis_index("depth")
    row_start, col_start = row_at * rows, lax.axis_index("col") * width
    main = width - width % LANES
    rem = width - main
    for k, (ref, fill_ref) in enumerate(((x_ref, fill_x_ref), (t_ref, fill_t_ref))):
        mask = block_fill(fill_ref, row_start, col_start, rows, width)
        masked = (ref[...].astype(jnp.float32) * mask).astype(out_ref.dtype)
        out_ref[0, :, k * main : (k + 1) * main] = masked[:, :main]
        if rem:
            out_ref[0, :, 2 * main + k * rem : 2 * main + (k + 1) * rem] = masked[:, main:]


def pick(value, which, total, width):
    main = width - width % LANES
    rem = width - main
    parts = [value[:, which * main : (which + 1) * main]]
    if rem:
        parts.append(value[:, total * main + which * rem : total * main + (which + 1) * rem])
    return jnp.concatenate(parts, axis=1) if rem else parts[0]


def place(bits, position):
    offset = 0
    for at, weight in bits:
        offset = offset + ((position >> at) & 1) * weight
    return offset


def walk(refs, step, carry):
    base = 0
    for ref in refs:
        count = ref.shape[0]
        if count <= 4:
            for i in range(count):
                carry = step(base + i, ref[i], carry)
        else:
            carry = lax.fori_loop(
                0, count, lambda i, c, ref=ref, base=base: step(base + i, ref[i], c), carry
            )
        base += count
    return carry


def first_kernel(counts, bits, width, *refs):
    n_rows, n_cols = counts
    left, right = refs[:n_rows], refs[n_rows : n_rows + n_cols]
    out_ref, lhs = refs[n_rows + n_cols :]
    row_bits, depth_bits, col_bits = bits
    rows = right[0].shape[1]
    parts = width // rows
    top = aligned(rows)
    main = width - width % LANES
    rem = width - main
    my_row, my_depth, my_col = (lax.axis_index(a) for a in ("row", "depth", "col"))
    layers = lax.axis_size("depth")

    def fill(position, block, carry):
        col = my_col ^ place(col_bits, position)
        for k in range(2):
            whole = pick(block, k, 2, width)
            for h in range(parts):
                lhs[col * parts + h, k * top : k * top + rows, :] = whole[:, h * rows : (h + 1) * rows]
        return carry

    walk(left, fill, 0)

    def multiply(position, block, carry):
        row = my_row ^ place(row_bits, position)
        depth = my_depth ^ place(depth_bits, position)
        return carry + jnp.dot(
            lhs[row * layers + depth], block, preferred_element_type=jnp.float32
        )

    acc = walk(right, multiply, jnp.zeros((lhs.shape[1], right[0].shape[2]), jnp.float32))
    for at, size, base in ((0, main, 0), (2 * main, rem, 3 * main)):
        if not size:
            continue
        square = acc[:rows, at : at + size]
        cross = acc[top : top + rows, at : at + size] + acc[:rows, at + size : at + 2 * size]
        high = cross.astype(jnp.bfloat16)
        low = (cross - high.astype(jnp.float32)).astype(jnp.bfloat16)
        for k, value in enumerate((high, low, square.astype(jnp.bfloat16))):
            out_ref[0, :, base + k * size : base + (k + 1) * size] = value


def last_kernel(counts, bits, width, *refs):
    n_rows, n_cols = counts
    left, right = refs[:n_rows], refs[n_rows : n_rows + n_cols]
    own_ref, out_ref, lhs = refs[n_rows + n_cols :]
    row_bits, depth_bits, col_bits = bits
    rows = right[0].shape[1]
    parts = width // rows
    top = aligned(rows)
    main = width - width % LANES
    rem = width - main
    my_row, my_depth, my_col = (lax.axis_index(a) for a in ("row", "depth", "col"))
    layers = lax.axis_size("depth")

    def fill(position, block, carry):
        col = my_col ^ place(col_bits, position)
        for k in range(3):
            whole = pick(block, k, 3, width)
            for h in range(parts):
                lhs[col * parts + h, k * top : k * top + rows, :] = whole[:, h * rows : (h + 1) * rows]
        return carry

    walk(left, fill, 0)

    def multiply(position, block, carry):
        row = my_row ^ place(row_bits, position)
        depth = my_depth ^ place(depth_bits, position)
        return carry + jnp.dot(
            lhs[row * layers + depth], block, preferred_element_type=jnp.float32
        )

    acc = walk(right, multiply, jnp.zeros((lhs.shape[1], right[0].shape[2]), jnp.float32))
    for at, size, base in ((0, main, 0), (2 * main, rem, main)):
        if not size:
            continue
        total = (
            acc[:rows, at : at + size]
            + acc[top : top + rows, at : at + size]
            + acc[2 * top : 2 * top + rows, at + size : at + 2 * size]
        )
        own = own_ref[0, :, at + size : at + 2 * size].astype(jnp.float32)
        out_ref[:, base : base + size] = 1.5 * own - 0.5 * total


def gather_columns(block):
    rows, layers = lax.axis_size("row"), lax.axis_size("depth")
    far = swap(block, "row", 3)
    near = swap(block, "row", 1)
    side = swap(block, "depth", 1)
    pair = jnp.concatenate([near, far], axis=0)
    opposite = swap(far, "row", 1)
    side_opposite = swap(side, "row", 2)
    side_pair = swap(pair, "depth", 1)
    row_bits, depth_bits = [(0, 1), (1, 2)], [(2, 1)]
    gathered = [block, near, opposite, far, side, side_pair[:1], side_opposite, side_pair[1:]]
    if rows == 4 and layers == 2:
        return gathered, row_bits, depth_bits
    held = jnp.concatenate(gathered, axis=0)
    at = 3
    for axis, offset, bits in [("row", 1 << k, row_bits) for k in range(2, rows.bit_length() - 1)] + [
        ("depth", 1 << k, depth_bits) for k in range(1, layers.bit_length() - 1)
    ]:
        held = jnp.concatenate([held, swap(held, axis, offset)], axis=0)
        bits.append((at, offset))
        at += 1
    return [held], row_bits, depth_bits


def gather_rows(block):
    size = lax.axis_size("col")
    bits, at, held = [], 0, block
    for k in range(1, size.bit_length() - 1):
        held = jnp.concatenate([held, swap(held, "col", 1 << k)], axis=0)
        bits.append((at, 1 << k))
        at += 1
    bits.append((at, 1))
    return [held, swap(held, "col", 1)], bits


def body(x_matrix, tangent, fill_x, fill_t):
    rows, width = x_matrix.shape
    main = width - width % LANES
    blocks = lax.axis_size("row") * lax.axis_size("depth")
    params = pltpu.CompilerParams(vmem_limit_bytes=LIMIT)
    packed = pl.pallas_call(
        pack_kernel,
        out_shape=jax.ShapeDtypeStruct((1, rows, 2 * width), jnp.bfloat16),
        in_specs=[VMEM, VMEM, SMEM, SMEM],
        out_specs=VMEM,
        compiler_params=params,
        name="pack",
    )(x_matrix, tangent, fill_x, fill_t)
    right, row_bits, depth_bits = gather_columns(packed)
    left, col_bits = gather_rows(packed)
    bits = (tuple(row_bits), tuple(depth_bits), tuple(col_bits))
    top = aligned(rows)
    firsts = pl.pallas_call(
        functools.partial(first_kernel, (len(left), len(right)), bits, width),
        out_shape=jax.ShapeDtypeStruct((1, rows, 3 * width), jnp.bfloat16),
        in_specs=[VMEM] * (len(left) + len(right)),
        out_specs=VMEM,
        scratch_shapes=[pltpu.VMEM((blocks, 2 * top, rows), jnp.bfloat16)],
        compiler_params=params,
        name="firsts",
    )(*left, *right)
    left, col_bits = gather_rows(firsts)
    return pl.pallas_call(
        functools.partial(last_kernel, (len(left), len(right)), bits, width),
        out_shape=jax.ShapeDtypeStruct((rows, width), jnp.float32),
        in_specs=[VMEM] * (len(left) + len(right) + 1),
        out_specs=VMEM,
        scratch_shapes=[pltpu.VMEM((blocks, 3 * top, rows), jnp.bfloat16)],
        compiler_params=params,
        name="lasts",
    )(*left, *right, packed)


def solution(mesh):
    placed = (P(("row", "depth"), "col"), P(("row", "depth"), "col"), P(), P())
    return jax.shard_map(
        body, mesh=mesh, in_specs=placed, out_specs=P(("row", "depth"), "col"), check_vma=False
    )
```

```python
import functools

import jax
import jax.numpy as jnp
from jax import lax
from jax.experimental import pallas as pl
from jax.experimental.pallas import tpu as pltpu
from jax.sharding import PartitionSpec as P

BLOCK = 128
LANES = 128
FOLD = 16
HBM = pl.BlockSpec(memory_space=pltpu.HBM)
VMEM = pl.BlockSpec(memory_space=pltpu.VMEM)
PARAMS = pltpu.CompilerParams(vmem_limit_bytes=48 * 1024 * 1024)


def aligned(rows):
    return -(-rows // 16) * 16


def split(width):
    rem = width % LANES
    return width - rem, rem, FOLD if rem else 0


def swap(value, axis, offset):
    size = lax.axis_size(axis)
    return lax.ppermute(value, axis, [(i, i ^ offset) for i in range(size)])


def block_fill(fill_ref, row_start, col_start, rows, width):
    count = fill_ref.shape[0]
    row_ids = row_start + lax.broadcasted_iota(jnp.int32, (rows, width), 0)
    col_ids = col_start + lax.broadcasted_iota(jnp.int32, (rows, width), 1)
    first_row, first_col = row_start // BLOCK, col_start // BLOCK
    mask = jnp.zeros((rows, width), jnp.float32)
    for i in range((rows - 2) // BLOCK + 2):
        row_at = first_row + i
        in_row = (row_ids >= row_at * BLOCK) & (row_ids < (row_at + 1) * BLOCK)
        for j in range((width - 2) // BLOCK + 2):
            col_at = first_col + j
            here = in_row & (col_ids >= col_at * BLOCK) & (col_ids < (col_at + 1) * BLOCK)
            flag = fill_ref[jnp.minimum(row_at, count - 1), jnp.minimum(col_at, count - 1)]
            mask = jnp.where(here, flag.astype(jnp.float32), mask)
    return mask


def fold(value):
    rows, lanes = value.shape
    spare = -rows % FOLD
    if spare:
        value = jnp.concatenate([value, jnp.zeros((spare, lanes), value.dtype)], axis=0)
    return jnp.concatenate([value[at : at + FOLD] for at in range(0, rows, FOLD)], axis=1)


def unfold(value, rows, lanes):
    groups = [value[:, k * lanes : (k + 1) * lanes] for k in range(-(-rows // FOLD))]
    return jnp.concatenate(groups, axis=0)[:rows]


def pack_kernel(
    x_hbm, t_hbm, fill_x_hbm, fill_t_hbm, out_ref, x_ref, t_ref, fill_x_ref, fill_t_ref, sems
):
    rows, width = x_ref.shape
    main, rem, lead = split(width)
    pairs = ((fill_x_hbm, fill_x_ref), (fill_t_hbm, fill_t_ref), (x_hbm, x_ref), (t_hbm, t_ref))
    copies = [pltpu.make_async_copy(src, dst, sems.at[k]) for k, (src, dst) in enumerate(pairs)]
    for copy in copies:
        copy.start()
    row_at = lax.axis_index("row") * lax.axis_size("depth") + lax.axis_index("depth")
    row_start, col_start = row_at * rows, lax.axis_index("col") * width
    copies[0].wait()
    copies[1].wait()
    masks = [block_fill(ref, row_start, col_start, rows, width) for ref in (fill_x_ref, fill_t_ref)]
    copies[2].wait()
    copies[3].wait()
    masked = [x_ref[...].astype(jnp.float32) * masks[0], t_ref[...].astype(jnp.float32) * masks[1]]
    for k, value in enumerate(masked):
        out_ref[0, lead:, k * main : (k + 1) * main] = value[:, :main].astype(out_ref.dtype)
    if rem:
        folded = fold(jnp.concatenate([value[:, main:] for value in masked], axis=1))
        out_ref[0, :FOLD, : folded.shape[1]] = folded.astype(out_ref.dtype)


def mains_and_rems(block, rows, rem, lead, total):
    mains = block[lead:]
    return mains, (unfold(block[:lead], rows, total * rem) if rem else None)


def place(bits, position):
    if isinstance(bits[0], int):
        return bits[position]
    offset = 0
    for at, weight in bits:
        offset = offset ^ (((position >> at) & 1) * weight)
    return offset


def walk(refs, step, carry):
    base = 0
    for ref in refs:
        count = ref.shape[0]
        if count <= 4:
            for i in range(count):
                carry = step(base + i, ref[i], carry)
        else:
            carry = lax.fori_loop(
                0, count, lambda i, c, ref=ref, base=base: step(base + i, ref[i], c), carry
            )
        base += count
    return carry


def panel_product(left, right, lhs, total, width, rows, places):
    row_bits, depth_bits, col_bits = places
    main, rem, lead = split(width)
    parts, top = width // rows, aligned(rows)
    my_row, my_depth, my_col = (lax.axis_index(a) for a in ("row", "depth", "col"))
    layers = lax.axis_size("depth")

    def fill(position, block, carry):
        col = my_col ^ place(col_bits, position)
        mains, rems = mains_and_rems(block, rows, rem, lead, total)
        for k in range(total):
            whole = mains[:, k * main : (k + 1) * main]
            if rem:
                whole = jnp.concatenate([whole, rems[:, k * rem : (k + 1) * rem]], axis=1)
            for h in range(parts):
                lhs[col * parts + h, k * top : k * top + rows, :] = whole[:, h * rows : (h + 1) * rows]
        return carry

    walk(left, fill, 0)

    def multiply(position, block, carry):
        row = my_row ^ place(row_bits, position)
        depth = my_depth ^ place(depth_bits, position)
        factor = lhs[row * layers + depth]
        operands = mains_and_rems(block, rows, rem, lead, 2)
        return tuple(
            c + jnp.dot(factor, o, preferred_element_type=jnp.float32)
            for c, o in zip(carry, operands[: len(carry)], strict=True)
        )

    sizes = (2 * main, 2 * rem) if rem else (2 * main,)
    zeros = tuple(jnp.zeros((lhs.shape[1], size), jnp.float32) for size in sizes)
    return walk(right, multiply, zeros)


def first_kernel(counts, places, width, *refs):
    n_left, n_right = counts
    left, right = refs[:n_left], refs[n_left : n_left + n_right]
    out_ref, lhs = refs[n_left + n_right :]
    main, rem, lead = split(width)
    rows = out_ref.shape[1] - lead
    top = aligned(rows)
    sums = panel_product(left, right, lhs, 2, width, rows, places)
    results = []
    for acc in sums:
        size = acc.shape[1] // 2
        square = acc[:rows, :size]
        cross = acc[top : top + rows, :size] + acc[:rows, size:]
        high = cross.astype(jnp.bfloat16).astype(jnp.float32)
        results.append((high, cross - high, square))
    for k, value in enumerate(results[0]):
        out_ref[0, lead:, k * main : (k + 1) * main] = value.astype(out_ref.dtype)
    if rem:
        folded = fold(jnp.concatenate(results[1], axis=1))
        out_ref[0, :FOLD, : folded.shape[1]] = folded.astype(out_ref.dtype)


def last_kernel(counts, places, width, *refs):
    n_left, n_right = counts
    left, right = refs[:n_left], refs[n_left : n_left + n_right]
    own_ref, out_ref, lhs = refs[n_left + n_right :]
    main, rem, lead = split(width)
    rows = out_ref.shape[0]
    top = aligned(rows)
    sums = panel_product(left, right, lhs, 3, width, rows, places)
    owns = mains_and_rems(own_ref[0], rows, rem, lead, 2)
    for acc, own, base in zip(sums, owns, (0, main)):
        size = acc.shape[1] // 2
        total = acc[:rows, :size] + acc[top : top + rows, :size] + acc[2 * top : 2 * top + rows, size:]
        out_ref[:, base : base + size] = 1.5 * own[:, size:].astype(jnp.float32) - 0.5 * total


def gather_columns(block):
    rows, layers = lax.axis_size("row"), lax.axis_size("depth")
    zs = [swap(block, "row", k) for k in (1, 2, 3)]
    line = jnp.concatenate([block] + zs, axis=0)
    gathered = [line, swap(line, "depth", 1)]
    row_bits, depth_bits = (0, 1, 2, 3, 0, 1, 2, 3), (0, 0, 0, 0, 1, 1, 1, 1)

    if rows == 4 and layers == 2:
        return gathered, row_bits, depth_bits
    places = list(zip(row_bits, depth_bits, strict=True))
    blocks = jnp.concatenate(gathered, axis=0)
    held = jnp.stack([blocks[places.index((k & 3, k >> 2))] for k in range(8)])
    row_bits, depth_bits, at = [(0, 1), (1, 2)], [(2, 1)], 3
    for axis, offset, bits in [("row", 1 << k, row_bits) for k in range(2, rows.bit_length() - 1)] + [
        ("depth", 1 << k, depth_bits) for k in range(1, layers.bit_length() - 1)
    ]:
        held = jnp.concatenate([held, swap(held, axis, offset)], axis=0)
        bits.append((at, offset))
        at += 1
    return [held], row_bits, depth_bits


def gather_rows(block):
    size = lax.axis_size("col")
    bits, at, held = [], 0, block
    for k in range(1, size.bit_length() - 1):
        held = jnp.concatenate([held, swap(held, "col", 1 << k)], axis=0)
        bits.append((at, 1 << k))
        at += 1
    bits.append((at, 1))
    return [held, swap(held, "col", 1)], bits


def body(x_matrix, tangent, fill_x, fill_t):
    rows, width = x_matrix.shape
    _, _, lead = split(width)
    blocks = lax.axis_size("row") * lax.axis_size("depth")
    packed = pl.pallas_call(
        pack_kernel,
        out_shape=jax.ShapeDtypeStruct((1, lead + rows, 2 * split(width)[0]), jnp.bfloat16),
        in_specs=[HBM] * 4,
        out_specs=VMEM,
        scratch_shapes=[
            pltpu.VMEM((rows, width), jnp.bfloat16),
            pltpu.VMEM((rows, width), jnp.bfloat16),
            pltpu.SMEM(fill_x.shape, jnp.int32),
            pltpu.SMEM(fill_t.shape, jnp.int32),
            pltpu.SemaphoreType.DMA((4,)),
        ],
        compiler_params=PARAMS,
        name="pack",
    )(*(pltpu.with_memory_space_constraint(a, pltpu.HBM) for a in (x_matrix, tangent, fill_x, fill_t)))
    right, row_bits, depth_bits = gather_columns(packed)
    left, col_bits = gather_rows(packed)
    places = (row_bits, depth_bits, col_bits)
    top = aligned(rows)
    firsts = pl.pallas_call(
        functools.partial(first_kernel, (len(left), len(right)), places, width),
        out_shape=jax.ShapeDtypeStruct((1, lead + rows, 3 * split(width)[0]), jnp.bfloat16),
        in_specs=[VMEM] * (len(left) + len(right)),
        out_specs=VMEM,
        scratch_shapes=[pltpu.VMEM((blocks, 2 * top, rows), jnp.bfloat16)],
        compiler_params=PARAMS,
        name="firsts",
    )(*left, *right)
    left, col_bits = gather_rows(firsts)
    return pl.pallas_call(
        functools.partial(last_kernel, (len(left), len(right)), places, width),
        out_shape=jax.ShapeDtypeStruct((rows, width), jnp.float32),
        in_specs=[VMEM] * (len(left) + len(right) + 1),
        out_specs=VMEM,
        scratch_shapes=[pltpu.VMEM((blocks, 3 * top, rows), jnp.bfloat16)],
        compiler_params=PARAMS,
        name="lasts",
    )(*left, *right, packed)


def solution(mesh):
    placed = (P(("row", "depth"), "col"), P(("row", "depth"), "col"), P(), P())
    return jax.shard_map(
        body, mesh=mesh, in_specs=placed, out_specs=P(("row", "depth"), "col"), check_vma=False
    )
```

```python
import functools

import jax
import jax.numpy as jnp
from jax import lax
from jax.experimental import pallas as pl
from jax.experimental.pallas import tpu as pltpu
from jax.sharding import PartitionSpec as P

BLOCK = 128
LANES = 128
FOLD = 16
HBM = pl.BlockSpec(memory_space=pltpu.HBM)
VMEM = pl.BlockSpec(memory_space=pltpu.VMEM)
PARAMS = pltpu.CompilerParams(vmem_limit_bytes=48 * 1024 * 1024)


def aligned(rows):
    return -(-rows // 16) * 16


def split(width):
    rem = width % LANES
    return width - rem, rem, FOLD if rem else 0


def swap(value, axis, offset):
    size = lax.axis_size(axis)
    return lax.ppermute(value, axis, [(i, i ^ offset) for i in range(size)])


def turn(value, axis, offset):
    size = lax.axis_size(axis)
    return lax.ppermute(value, axis, [((i + offset) % size, i) for i in range(size)])


def block_fill(fill_ref, row_start, col_start, rows, width):
    count = fill_ref.shape[0]
    row_ids = row_start + lax.broadcasted_iota(jnp.int32, (rows, width), 0)
    col_ids = col_start + lax.broadcasted_iota(jnp.int32, (rows, width), 1)
    first_row, first_col = row_start // BLOCK, col_start // BLOCK
    mask = jnp.zeros((rows, width), jnp.float32)
    for i in range((rows - 2) // BLOCK + 2):
        row_at = first_row + i
        in_row = (row_ids >= row_at * BLOCK) & (row_ids < (row_at + 1) * BLOCK)
        for j in range((width - 2) // BLOCK + 2):
            col_at = first_col + j
            here = in_row & (col_ids >= col_at * BLOCK) & (col_ids < (col_at + 1) * BLOCK)
            flag = fill_ref[jnp.minimum(row_at, count - 1), jnp.minimum(col_at, count - 1)]
            mask = jnp.where(here, flag.astype(jnp.float32), mask)
    return mask


def fold(value):
    rows, lanes = value.shape
    spare = -rows % FOLD
    if spare:
        value = jnp.concatenate([value, jnp.zeros((spare, lanes), value.dtype)], axis=0)
    return jnp.concatenate([value[at : at + FOLD] for at in range(0, rows, FOLD)], axis=1)


def unfold(value, rows, lanes):
    groups = [value[:, k * lanes : (k + 1) * lanes] for k in range(-(-rows // FOLD))]
    return jnp.concatenate(groups, axis=0)[:rows]


def pack_kernel(
    x_hbm, t_hbm, fill_x_hbm, fill_t_hbm, out_ref, x_ref, t_ref, fill_x_ref, fill_t_ref, sems
):
    rows, width = x_ref.shape
    pairs = ((fill_x_hbm, fill_x_ref), (fill_t_hbm, fill_t_ref), (x_hbm, x_ref), (t_hbm, t_ref))
    copies = [pltpu.make_async_copy(src, dst, sems.at[k]) for k, (src, dst) in enumerate(pairs)]
    for copy in copies:
        copy.start()
    row_at = lax.axis_index("row") * lax.axis_size("depth") + lax.axis_index("depth")
    row_start, col_start = row_at * rows, lax.axis_index("col") * width
    copies[0].wait()
    copies[1].wait()
    masks = [block_fill(ref, row_start, col_start, rows, width) for ref in (fill_x_ref, fill_t_ref)]
    copies[2].wait()
    copies[3].wait()
    masked = [x_ref[...].astype(jnp.float32) * masks[0], t_ref[...].astype(jnp.float32) * masks[1]]
    pack(out_ref, masked, width)


def natural(block, rows, width, total):
    main, rem, lead = split(width)
    parts = [block[lead : lead + rows, k * main : (k + 1) * main] for k in range(total)]
    if rem:
        rems = unfold(block[:lead], rows, total * rem)
        parts = [
            jnp.concatenate([part, rems[:, k * rem : (k + 1) * rem]], axis=1)
            for k, part in enumerate(parts)
        ]
    return parts


def pack(out_ref, values, width):
    main, rem, lead = split(width)
    for k, value in enumerate(values):
        out_ref[0, lead:, k * main : (k + 1) * main] = value[:, :main].astype(out_ref.dtype)
    if rem:
        folded = fold(jnp.concatenate([value[:, main:] for value in values], axis=1))
        out_ref[0, :lead, : folded.shape[1]] = folded.astype(out_ref.dtype)


def mains_and_rems(block, rows, rem, lead, total):
    mains = block[lead:]
    return mains, (unfold(block[:lead], rows, total * rem) if rem else None)


def place(bits, position):
    offset = 0
    for at, weight in bits:
        offset = offset ^ (((position >> at) & 1) * weight)
    return offset


def walk(refs, step, carry):
    base = 0
    for ref in refs:
        count = ref.shape[0]
        if count <= 4:
            for i in range(count):
                carry = step(base + i, ref[i], carry)
        else:
            carry = lax.fori_loop(
                0, count, lambda i, c, ref=ref, base=base: step(base + i, ref[i], c), carry
            )
        base += count
    return carry


def panel_product(left, right, lhs, total, width, rows, places):
    row_bits, depth_bits, col_bits = places
    main, rem, lead = split(width)
    parts, top = width // rows, aligned(rows)
    my_row, my_depth, my_col = (lax.axis_index(a) for a in ("row", "depth", "col"))
    layers = lax.axis_size("depth")

    def fill(position, block, carry):
        col = my_col ^ place(col_bits, position)
        mains, rems = mains_and_rems(block, rows, rem, lead, total)
        for k in range(total):
            whole = mains[:, k * main : (k + 1) * main]
            if rem:
                whole = jnp.concatenate([whole, rems[:, k * rem : (k + 1) * rem]], axis=1)
            for h in range(parts):
                lhs[col * parts + h, k * top : k * top + rows, :] = whole[:, h * rows : (h + 1) * rows]
        return carry

    walk(left, fill, 0)

    def multiply(position, block, carry):
        row = my_row ^ place(row_bits, position)
        depth = my_depth ^ place(depth_bits, position)
        factor = lhs[row * layers + depth]
        operands = mains_and_rems(block, rows, rem, lead, 2)
        return tuple(
            c + jnp.dot(factor, o, preferred_element_type=jnp.float32)
            for c, o in zip(carry, operands[: len(carry)], strict=True)
        )

    sizes = (2 * main, 2 * rem) if rem else (2 * main,)
    zeros = tuple(jnp.zeros((lhs.shape[1], size), jnp.float32) for size in sizes)
    return walk(right, multiply, zeros)


def first_kernel(counts, places, width, *refs):
    n_left, n_right = counts
    left, right = refs[:n_left], refs[n_left : n_left + n_right]
    out_ref, lhs = refs[n_left + n_right :]
    main, rem, lead = split(width)
    rows = out_ref.shape[1] - lead
    top = aligned(rows)
    sums = panel_product(left, right, lhs, 2, width, rows, places)
    results = []
    for acc in sums:
        size = acc.shape[1] // 2
        square = acc[:rows, :size]
        cross = acc[top : top + rows, :size] + acc[:rows, size:]
        high = cross.astype(jnp.bfloat16).astype(jnp.float32)
        results.append((high, cross - high, square))
    for k, value in enumerate(results[0]):
        out_ref[0, lead:, k * main : (k + 1) * main] = value.astype(out_ref.dtype)
    if rem:
        folded = fold(jnp.concatenate(results[1], axis=1))
        out_ref[0, :FOLD, : folded.shape[1]] = folded.astype(out_ref.dtype)


def last_kernel(counts, places, width, *refs):
    n_left, n_right = counts
    left, right = refs[:n_left], refs[n_left : n_left + n_right]
    own_ref, out_ref, lhs = refs[n_left + n_right :]
    main, rem, lead = split(width)
    rows = out_ref.shape[0]
    top = aligned(rows)
    sums = panel_product(left, right, lhs, 3, width, rows, places)
    owns = mains_and_rems(own_ref[0], rows, rem, lead, 2)
    for acc, own, base in zip(sums, owns, (0, main)):
        size = acc.shape[1] // 2
        total = acc[:rows, :size] + acc[top : top + rows, :size] + acc[2 * top : 2 * top + rows, size:]
        out_ref[:, base : base + size] = 1.5 * own[:, size:].astype(jnp.float32) - 0.5 * total


def times(left, right):
    return jnp.dot(left, right, preferred_element_type=jnp.float32)


def add_panels(offsets, mine, others, lhs, rhs, width, rows):
    my_row, my_depth = lax.axis_index("row"), lax.axis_index("depth")
    top = aligned(rows)
    square = cross = jnp.zeros((rows, width), jnp.float32)
    for k, offset in enumerate(offsets):
        row = lax.rem(my_row + offset, lax.axis_size("row"))
        panels = []
        for a, b in zip(
            natural(mine[k], rows, width, 2), natural(others[k], rows, width, 2), strict=True
        ):
            a, b = a.astype(jnp.float32), b.astype(jnp.float32)
            halves = [jnp.where(my_depth == 0, a, b), jnp.where(my_depth == 0, b, a)]
            panels.append(jnp.concatenate(halves, axis=0).astype(jnp.bfloat16))
        for which, panel in enumerate(panels):
            rhs[row, which] = panel
        both = times(lhs[row], panels[0])
        square += both[:rows]
        cross += both[top : top + rows] + times(lhs[row, :rows], panels[1])
    return square, cross


def firsts_kernel(offsets, width, own, beside, *refs):
    mine, others = refs[: len(offsets)], refs[len(offsets) : 2 * len(offsets)]
    out_ref, low_ref, rhs, lhs = refs[2 * len(offsets) :]
    rows = own.shape[1] - split(width)[2]
    top = aligned(rows)
    my_col = lax.axis_index("col")
    for ref, across in ((own, 0), (beside, 1)):
        for k in range(2):
            col = my_col ^ across ^ (3 * k)
            for which, part in enumerate(natural(ref[k], rows, width, 2)):
                lhs[col, which * top : which * top + rows, :] = part
    square = cross = jnp.zeros((rows, width), jnp.float32)
    for row_offsets, left, right in zip(offsets, mine, others, strict=True):
        terms = add_panels(row_offsets, left, right, lhs, rhs, width, rows)
        square, cross = square + terms[0], cross + terms[1]
    high = cross.astype(jnp.bfloat16).astype(jnp.float32)
    pack(out_ref, (high, square), width)
    low_ref[...] = jnp.zeros_like(low_ref)
    pack(low_ref, (cross - high,), width)


def panel_terms(col, block, low, rhs, width, rows):
    high, square = natural(block, rows, width, 2)
    total = times(high, rhs[col, 0]) + times(square, rhs[col, 1])
    if low is not None:
        total += times(natural(low, rows, width, 1)[0], rhs[col, 0])
    return total


def early_lasts_kernel(width, held, rhs, out_ref):
    rows = out_ref.shape[0]
    my_col = lax.axis_index("col")
    out_ref[...] = panel_terms(my_col, held[0], held[2], rhs, width, rows) + panel_terms(
        my_col ^ 3, held[1], None, rhs, width, rows
    )


def late_lasts_kernel(width, other, rhs, early, own_ref, out_ref):
    rows = out_ref.shape[0]
    my_col = lax.axis_index("col")
    total = early[...] + panel_terms(my_col ^ 1, other[0], other[2], rhs, width, rows)
    total += panel_terms(my_col ^ 2, other[1], None, rhs, width, rows)
    own = natural(own_ref[0], rows, width, 2)[1].astype(jnp.float32)
    out_ref[...] = 1.5 * own - 0.5 * total


def call(kernel, name, out_shape, operands, scratch=(), **kwargs):
    return pl.pallas_call(
        kernel,
        out_shape=out_shape,
        in_specs=[VMEM] * len(operands),
        out_specs=jax.tree.map(lambda _: VMEM, out_shape),
        scratch_shapes=list(scratch),
        compiler_params=PARAMS,
        name=name,
        **kwargs,
    )(*operands)


def fast_body(block, rows, width):
    grid, top = lax.axis_size("row"), aligned(rows)
    shape = jax.ShapeDtypeStruct
    opposite = turn(block, "row", 2)
    line = jnp.concatenate([turn(block, "row", 1), turn(block, "row", 3), block], axis=0)
    side_line = swap(line, "depth", 1)
    side_opposite = swap(opposite, "depth", 1)
    held = jnp.concatenate([block, swap(block, "col", 3)], axis=0)
    beside = swap(held, "col", 1)
    panels = shape((grid, 2, width, width), jnp.bfloat16)
    firsts, low, rhs = call(
        functools.partial(firsts_kernel, ((1, 3, 0), (2,)), width),
        "firsts",
        (shape(block.shape, block.dtype), shape(block.shape, block.dtype), panels),
        (held, beside, line, opposite, side_line, side_opposite),
        [pltpu.VMEM((grid, 2 * top, width), jnp.bfloat16)],
    )
    held = jnp.concatenate([firsts, swap(firsts, "col", 3), low], axis=0)
    other = swap(held, "col", 1)
    out = shape((rows, width), jnp.float32)
    early = call(
        functools.partial(early_lasts_kernel, width), "early_lasts", out, (held, rhs)
    )
    return call(
        functools.partial(late_lasts_kernel, width), "late_lasts", out, (other, rhs, early, block)
    )


def gather(block, axes):
    held, at, bits = block, 0, []
    for axis, steps in axes:
        meaning = []
        for step in steps:
            held = jnp.concatenate([held, swap(held, axis, step)], axis=0)
            meaning.append((at, step))
            at += 1
        bits.append(meaning)
    return [held], bits


def general_body(block, rows, width):
    def steps(axis):
        return [1 << k for k in range(lax.axis_size(axis).bit_length() - 1)]

    right, (row_bits, depth_bits) = gather(block, [(a, steps(a)) for a in ("row", "depth")])
    left, (col_bits,) = gather(block, [("col", steps("col")[::-1])])
    places = (row_bits, depth_bits, col_bits)
    blocks, top = right[0].shape[0], aligned(rows)
    _, _, lead = split(width)
    firsts = call(
        functools.partial(first_kernel, (1, 1), places, width),
        "firsts",
        jax.ShapeDtypeStruct((1, lead + rows, 3 * split(width)[0]), jnp.bfloat16),
        (*left, *right),
        [pltpu.VMEM((blocks, 2 * top, rows), jnp.bfloat16)],
    )
    left, (col_bits,) = gather(firsts, [("col", steps("col")[::-1])])
    return call(
        functools.partial(last_kernel, (1, 1), places, width),
        "lasts",
        jax.ShapeDtypeStruct((rows, width), jnp.float32),
        (*left, *right, block),
        [pltpu.VMEM((blocks, 3 * top, rows), jnp.bfloat16)],
    )


def body(x_matrix, tangent, fill_x, fill_t):
    rows, width = x_matrix.shape
    main, _, lead = split(width)
    block = pl.pallas_call(
        pack_kernel,
        out_shape=jax.ShapeDtypeStruct((1, lead + rows, 2 * main), jnp.bfloat16),
        in_specs=[HBM] * 4,
        out_specs=VMEM,
        scratch_shapes=[
            pltpu.VMEM((rows, width), jnp.bfloat16),
            pltpu.VMEM((rows, width), jnp.bfloat16),
            pltpu.SMEM(fill_x.shape, jnp.int32),
            pltpu.SMEM(fill_t.shape, jnp.int32),
            pltpu.SemaphoreType.DMA((4,)),
        ],
        compiler_params=PARAMS,
        name="pack",
    )(*(pltpu.with_memory_space_constraint(a, pltpu.HBM) for a in (x_matrix, tangent, fill_x, fill_t)))
    sizes = tuple(lax.axis_size(a) for a in ("row", "col", "depth"))
    return (fast_body if sizes == (4, 4, 2) else general_body)(block, rows, width)


def solution(mesh):
    placed = (P(("row", "depth"), "col"), P(("row", "depth"), "col"), P(), P())
    return jax.shard_map(
        body, mesh=mesh, in_specs=placed, out_specs=P(("row", "depth"), "col"), check_vma=False
    )
```

```python
import functools

import jax
import jax.numpy as jnp
from jax import lax
from jax.experimental import pallas as pl
from jax.experimental.pallas import tpu as pltpu
from jax.sharding import PartitionSpec as P

BLOCK = 128
LANES = 128
FOLD = 16
HBM = pl.BlockSpec(memory_space=pltpu.HBM)
VMEM = pl.BlockSpec(memory_space=pltpu.VMEM)
PARAMS = pltpu.CompilerParams(vmem_limit_bytes=48 * 1024 * 1024)


def aligned(rows):
    return -(-rows // 16) * 16


def split(width):
    rem = width % LANES
    return width - rem, rem, FOLD if rem else 0


def swap(value, axis, offset):
    size = lax.axis_size(axis)
    return lax.ppermute(value, axis, [(i, i ^ offset) for i in range(size)])


def turn(value, axis, offset):
    size = lax.axis_size(axis)
    return lax.ppermute(value, axis, [((i + offset) % size, i) for i in range(size)])


def block_fill(fill_ref, row_start, col_start, rows, width):
    count = fill_ref.shape[0]
    row_ids = row_start + lax.broadcasted_iota(jnp.int32, (rows, width), 0)
    col_ids = col_start + lax.broadcasted_iota(jnp.int32, (1, width), 1)
    first_row, first_col = row_start // BLOCK, col_start // BLOCK
    mask = None
    for i in range((rows - 2) // BLOCK + 2):
        row_at = jnp.minimum(first_row + i, count - 1)
        flags = None
        for j in range((width - 2) // BLOCK + 2):
            flag = fill_ref[row_at, jnp.minimum(first_col + j, count - 1)].astype(jnp.float32)
            passed = col_ids >= (first_col + j) * BLOCK
            flags = jnp.where(passed, flag, 0.0 if flags is None else flags)
        flags = jnp.broadcast_to(flags, (rows, width))
        mask = flags if mask is None else jnp.where(row_ids >= (first_row + i) * BLOCK, flags, mask)
    return mask


def fold(value):
    rows, lanes = value.shape
    spare = -rows % FOLD
    if spare:
        value = jnp.concatenate([value, jnp.zeros((spare, lanes), value.dtype)], axis=0)
    return jnp.concatenate([value[at : at + FOLD] for at in range(0, rows, FOLD)], axis=1)


def unfold(value, rows, lanes):
    groups = [value[:, k * lanes : (k + 1) * lanes] for k in range(-(-rows // FOLD))]
    return jnp.concatenate(groups, axis=0)[:rows]


def pack_kernel(
    x_hbm, t_hbm, fill_x_hbm, fill_t_hbm, out_ref, x_ref, t_ref, fill_x_ref, fill_t_ref, sems
):
    rows, width = x_ref.shape
    pairs = ((fill_x_hbm, fill_x_ref), (fill_t_hbm, fill_t_ref), (x_hbm, x_ref), (t_hbm, t_ref))
    copies = [pltpu.make_async_copy(src, dst, sems.at[k]) for k, (src, dst) in enumerate(pairs)]
    for copy in copies:
        copy.start()
    row_at = lax.axis_index("row") * lax.axis_size("depth") + lax.axis_index("depth")
    row_start, col_start = row_at * rows, lax.axis_index("col") * width
    copies[0].wait()
    copies[1].wait()
    masks = [block_fill(ref, row_start, col_start, rows, width) for ref in (fill_x_ref, fill_t_ref)]
    copies[2].wait()
    copies[3].wait()
    masked = [x_ref[...].astype(jnp.float32) * masks[0], t_ref[...].astype(jnp.float32) * masks[1]]
    pack(out_ref, masked, width)


def natural(block, rows, width, total):
    main, rem, lead = split(width)
    parts = [block[lead : lead + rows, k * main : (k + 1) * main] for k in range(total)]
    if rem:
        rems = unfold(block[:lead], rows, total * rem)
        parts = [
            jnp.concatenate([part, rems[:, k * rem : (k + 1) * rem]], axis=1)
            for k, part in enumerate(parts)
        ]
    return parts


def pack(out_ref, values, width):
    main, rem, lead = split(width)
    for k, value in enumerate(values):
        out_ref[0, lead:, k * main : (k + 1) * main] = value[:, :main].astype(out_ref.dtype)
    if rem:
        folded = fold(jnp.concatenate([value[:, main:] for value in values], axis=1))
        out_ref[0, :lead, : folded.shape[1]] = folded.astype(out_ref.dtype)


def mains_and_rems(block, rows, rem, lead, total):
    mains = block[lead:]
    return mains, (unfold(block[:lead], rows, total * rem) if rem else None)


def place(bits, position):
    offset = 0
    for at, weight in bits:
        offset = offset ^ (((position >> at) & 1) * weight)
    return offset


def walk(refs, step, carry):
    base = 0
    for ref in refs:
        count = ref.shape[0]
        if count <= 4:
            for i in range(count):
                carry = step(base + i, ref[i], carry)
        else:
            carry = lax.fori_loop(
                0, count, lambda i, c, ref=ref, base=base: step(base + i, ref[i], c), carry
            )
        base += count
    return carry


def panel_product(left, right, lhs, total, width, rows, places):
    row_bits, depth_bits, col_bits = places
    main, rem, lead = split(width)
    parts, top = width // rows, aligned(rows)
    my_row, my_depth, my_col = (lax.axis_index(a) for a in ("row", "depth", "col"))
    layers = lax.axis_size("depth")

    def fill(position, block, carry):
        col = my_col ^ place(col_bits, position)
        mains, rems = mains_and_rems(block, rows, rem, lead, total)
        for k in range(total):
            whole = mains[:, k * main : (k + 1) * main]
            if rem:
                whole = jnp.concatenate([whole, rems[:, k * rem : (k + 1) * rem]], axis=1)
            for h in range(parts):
                lhs[col * parts + h, k * top : k * top + rows, :] = whole[:, h * rows : (h + 1) * rows]
        return carry

    walk(left, fill, 0)

    def multiply(position, block, carry):
        row = my_row ^ place(row_bits, position)
        depth = my_depth ^ place(depth_bits, position)
        factor = lhs[row * layers + depth]
        operands = mains_and_rems(block, rows, rem, lead, 2)
        return tuple(
            c + jnp.dot(factor, o, preferred_element_type=jnp.float32)
            for c, o in zip(carry, operands[: len(carry)], strict=True)
        )

    sizes = (2 * main, 2 * rem) if rem else (2 * main,)
    zeros = tuple(jnp.zeros((lhs.shape[1], size), jnp.float32) for size in sizes)
    return walk(right, multiply, zeros)


def first_kernel(counts, places, width, *refs):
    n_left, n_right = counts
    left, right = refs[:n_left], refs[n_left : n_left + n_right]
    out_ref, lhs = refs[n_left + n_right :]
    main, rem, lead = split(width)
    rows = out_ref.shape[1] - lead
    top = aligned(rows)
    sums = panel_product(left, right, lhs, 2, width, rows, places)
    results = []
    for acc in sums:
        size = acc.shape[1] // 2
        square = acc[:rows, :size]
        cross = acc[top : top + rows, :size] + acc[:rows, size:]
        high = cross.astype(jnp.bfloat16).astype(jnp.float32)
        results.append((high, cross - high, square))
    for k, value in enumerate(results[0]):
        out_ref[0, lead:, k * main : (k + 1) * main] = value.astype(out_ref.dtype)
    if rem:
        folded = fold(jnp.concatenate(results[1], axis=1))
        out_ref[0, :FOLD, : folded.shape[1]] = folded.astype(out_ref.dtype)


def last_kernel(counts, places, width, *refs):
    n_left, n_right = counts
    left, right = refs[:n_left], refs[n_left : n_left + n_right]
    own_ref, out_ref, lhs = refs[n_left + n_right :]
    main, rem, lead = split(width)
    rows = out_ref.shape[0]
    top = aligned(rows)
    sums = panel_product(left, right, lhs, 3, width, rows, places)
    owns = mains_and_rems(own_ref[0], rows, rem, lead, 2)
    for acc, own, base in zip(sums, owns, (0, main)):
        size = acc.shape[1] // 2
        total = acc[:rows, :size] + acc[top : top + rows, :size] + acc[2 * top : 2 * top + rows, size:]
        out_ref[:, base : base + size] = 1.5 * own[:, size:].astype(jnp.float32) - 0.5 * total


def times(left, right):
    return jnp.dot(left, right, preferred_element_type=jnp.float32)


def add_panels(offsets, mine, others, lhs, rhs, width, rows):
    my_row, my_depth = lax.axis_index("row"), lax.axis_index("depth")
    top = aligned(rows)
    square = cross = jnp.zeros((rows, width), jnp.float32)
    for k, offset in enumerate(offsets):
        row = lax.rem(my_row + offset, lax.axis_size("row"))
        panels = []
        for a, b in zip(
            natural(mine[k], rows, width, 2), natural(others[k], rows, width, 2), strict=True
        ):
            a, b = a.astype(jnp.float32), b.astype(jnp.float32)
            halves = [jnp.where(my_depth == 0, a, b), jnp.where(my_depth == 0, b, a)]
            panels.append(jnp.concatenate(halves, axis=0).astype(jnp.bfloat16))
        for which, panel in enumerate(panels):
            rhs[row, which] = panel
        both = times(lhs[row], panels[0])
        square += both[:rows]
        cross += both[top : top + rows] + times(lhs[row, :rows], panels[1])
    return square, cross


def firsts_kernel(offsets, width, own, beside, *refs):
    mine, others = refs[: len(offsets)], refs[len(offsets) : 2 * len(offsets)]
    out_ref, low_ref, rhs, lhs = refs[2 * len(offsets) :]
    rows = own.shape[1] - split(width)[2]
    top = aligned(rows)
    my_col = lax.axis_index("col")
    for ref, across in ((own, 0), (beside, 1)):
        for k in range(2):
            col = my_col ^ across ^ (3 * k)
            for which, part in enumerate(natural(ref[k], rows, width, 2)):
                lhs[col, which * top : which * top + rows, :] = part
    square = cross = jnp.zeros((rows, width), jnp.float32)
    for row_offsets, left, right in zip(offsets, mine, others, strict=True):
        terms = add_panels(row_offsets, left, right, lhs, rhs, width, rows)
        square, cross = square + terms[0], cross + terms[1]
    high = cross.astype(jnp.bfloat16).astype(jnp.float32)
    pack(out_ref, (high, square), width)
    low_ref[...] = jnp.zeros_like(low_ref)
    pack(low_ref, (cross - high,), width)


def panel_terms(col, block, low, rhs, width, rows):
    high, square = natural(block, rows, width, 2)
    total = times(high, rhs[col, 0]) + times(square, rhs[col, 1])
    if low is not None:
        total += times(natural(low, rows, width, 1)[0], rhs[col, 0])
    return total


def near_lasts_kernel(width, mine, other, rhs, out_ref):
    rows = out_ref.shape[0]
    my_col = lax.axis_index("col")
    out_ref[...] = panel_terms(my_col, mine[0], mine[1], rhs, width, rows) + panel_terms(
        my_col ^ 1, other[0], other[1], rhs, width, rows
    )


def far_lasts_kernel(width, across, rhs, early, out_ref):
    rows = out_ref.shape[0]
    my_col = lax.axis_index("col")
    out_ref[...] = early[...] + panel_terms(my_col ^ 3, across[0], None, rhs, width, rows)


def late_lasts_kernel(width, across, rhs, early, own_ref, out_ref):
    rows = out_ref.shape[0]
    my_col = lax.axis_index("col")
    total = early[...] + panel_terms(my_col ^ 2, across[0], None, rhs, width, rows)
    own = natural(own_ref[0], rows, width, 2)[1].astype(jnp.float32)
    out_ref[...] = 1.5 * own - 0.5 * total


def call(kernel, name, out_shape, operands, scratch=(), **kwargs):
    return pl.pallas_call(
        kernel,
        out_shape=out_shape,
        in_specs=[VMEM] * len(operands),
        out_specs=jax.tree.map(lambda _: VMEM, out_shape),
        scratch_shapes=list(scratch),
        compiler_params=PARAMS,
        name=name,
        **kwargs,
    )(*operands)


def fast_body(block, rows, width):
    grid, top = lax.axis_size("row"), aligned(rows)
    shape = jax.ShapeDtypeStruct
    opposite = turn(block, "row", 2)
    line = jnp.concatenate([turn(block, "row", 1), turn(block, "row", 3), block], axis=0)
    side_line = swap(line, "depth", 1)
    side_opposite = swap(opposite, "depth", 1)
    held = jnp.concatenate([block, swap(block, "col", 3)], axis=0)
    beside = swap(held, "col", 1)
    panels = shape((grid, 2, width, width), jnp.bfloat16)
    firsts, low, rhs = call(
        functools.partial(firsts_kernel, ((1, 3, 0), (2,)), width),
        "firsts",
        (shape(block.shape, block.dtype), shape(block.shape, block.dtype), panels),
        (held, beside, line, opposite, side_line, side_opposite),
        [pltpu.VMEM((grid, 2 * top, width), jnp.bfloat16)],
    )
    across = swap(firsts, "col", 3)
    out = shape((rows, width), jnp.float32)
    mine = jnp.concatenate([firsts, low], axis=0)
    near = (mine, swap(mine, "col", 1))
    total = call(functools.partial(near_lasts_kernel, width), "near_lasts", out, (*near, rhs))
    total = call(functools.partial(far_lasts_kernel, width), "far_lasts", out, (across, rhs, total))
    return call(
        functools.partial(late_lasts_kernel, width),
        "late_lasts",
        out,
        (swap(across, "col", 1), rhs, total, block),
    )


def gather(block, axes):
    held, at, bits = block, 0, []
    for axis, steps in axes:
        meaning = []
        for step in steps:
            held = jnp.concatenate([held, swap(held, axis, step)], axis=0)
            meaning.append((at, step))
            at += 1
        bits.append(meaning)
    return [held], bits


def general_body(block, rows, width):
    def steps(axis):
        return [1 << k for k in range(lax.axis_size(axis).bit_length() - 1)]

    right, (row_bits, depth_bits) = gather(block, [(a, steps(a)) for a in ("row", "depth")])
    left, (col_bits,) = gather(block, [("col", steps("col")[::-1])])
    places = (row_bits, depth_bits, col_bits)
    blocks, top = right[0].shape[0], aligned(rows)
    _, _, lead = split(width)
    firsts = call(
        functools.partial(first_kernel, (1, 1), places, width),
        "firsts",
        jax.ShapeDtypeStruct((1, lead + rows, 3 * split(width)[0]), jnp.bfloat16),
        (*left, *right),
        [pltpu.VMEM((blocks, 2 * top, rows), jnp.bfloat16)],
    )
    left, (col_bits,) = gather(firsts, [("col", steps("col")[::-1])])
    return call(
        functools.partial(last_kernel, (1, 1), places, width),
        "lasts",
        jax.ShapeDtypeStruct((rows, width), jnp.float32),
        (*left, *right, block),
        [pltpu.VMEM((blocks, 3 * top, rows), jnp.bfloat16)],
    )


def body(x_matrix, tangent, fill_x, fill_t):
    rows, width = x_matrix.shape
    main, _, lead = split(width)
    block = pl.pallas_call(
        pack_kernel,
        out_shape=jax.ShapeDtypeStruct((1, lead + rows, 2 * main), jnp.bfloat16),
        in_specs=[HBM] * 4,
        out_specs=VMEM,
        scratch_shapes=[
            pltpu.VMEM((rows, width), jnp.bfloat16),
            pltpu.VMEM((rows, width), jnp.bfloat16),
            pltpu.SMEM(fill_x.shape, jnp.int32),
            pltpu.SMEM(fill_t.shape, jnp.int32),
            pltpu.SemaphoreType.DMA((4,)),
        ],
        compiler_params=PARAMS,
        name="pack",
    )(*(pltpu.with_memory_space_constraint(a, pltpu.HBM) for a in (x_matrix, tangent, fill_x, fill_t)))
    sizes = tuple(lax.axis_size(a) for a in ("row", "col", "depth"))
    return (fast_body if sizes == (4, 4, 2) else general_body)(block, rows, width)


def solution(mesh):
    placed = (P(("row", "depth"), "col"), P(("row", "depth"), "col"), P(), P())
    return jax.shard_map(
        body, mesh=mesh, in_specs=placed, out_specs=P(("row", "depth"), "col"), check_vma=False
    )
```

```python
import functools

import jax
import jax.numpy as jnp
from jax import lax
from jax.experimental import pallas as pl
from jax.experimental.pallas import tpu as pltpu
from jax.sharding import PartitionSpec as P

BLOCK = 128
LANES = 128
FOLD = 16
HBM = pl.BlockSpec(memory_space=pltpu.HBM)
VMEM = pl.BlockSpec(memory_space=pltpu.VMEM)
PARAMS = pltpu.CompilerParams(vmem_limit_bytes=48 * 1024 * 1024)


def aligned(rows):
    return -(-rows // 16) * 16


def split(width):
    rem = width % LANES
    return width - rem, rem, FOLD if rem else 0


def swap(value, axis, offset):
    size = lax.axis_size(axis)
    return lax.ppermute(value, axis, [(i, i ^ offset) for i in range(size)])


def turn(value, axis, offset):
    size = lax.axis_size(axis)
    return lax.ppermute(value, axis, [((i + offset) % size, i) for i in range(size)])


def block_fill(fill_ref, row_start, col_start, rows, width):
    count = fill_ref.shape[0]
    row_ids = row_start + lax.broadcasted_iota(jnp.int32, (rows, width), 0)
    col_ids = col_start + lax.broadcasted_iota(jnp.int32, (1, width), 1)
    first_row, first_col = row_start // BLOCK, col_start // BLOCK
    mask = None
    for i in range((rows - 2) // BLOCK + 2):
        row_at = jnp.minimum(first_row + i, count - 1)
        flags = None
        for j in range((width - 2) // BLOCK + 2):
            flag = fill_ref[row_at, jnp.minimum(first_col + j, count - 1)].astype(jnp.float32)
            passed = col_ids >= (first_col + j) * BLOCK
            flags = jnp.where(passed, flag, 0.0 if flags is None else flags)
        flags = jnp.broadcast_to(flags, (rows, width))
        mask = flags if mask is None else jnp.where(row_ids >= (first_row + i) * BLOCK, flags, mask)
    return mask


def fold(value):
    rows, lanes = value.shape
    spare = -rows % FOLD
    if spare:
        value = jnp.concatenate([value, jnp.zeros((spare, lanes), value.dtype)], axis=0)
    return jnp.concatenate([value[at : at + FOLD] for at in range(0, rows, FOLD)], axis=1)


def unfold(value, rows, lanes):
    groups = [value[:, k * lanes : (k + 1) * lanes] for k in range(-(-rows // FOLD))]
    return jnp.concatenate(groups, axis=0)[:rows]


def pack_kernel(
    x_hbm, t_hbm, fill_x_hbm, fill_t_hbm, out_ref, x_ref, t_ref, fill_x_ref, fill_t_ref, sems
):
    rows, width = x_ref.shape
    pairs = ((fill_x_hbm, fill_x_ref), (fill_t_hbm, fill_t_ref), (x_hbm, x_ref), (t_hbm, t_ref))
    copies = [pltpu.make_async_copy(src, dst, sems.at[k]) for k, (src, dst) in enumerate(pairs)]
    for copy in copies:
        copy.start()
    row_at = lax.axis_index("row") * lax.axis_size("depth") + lax.axis_index("depth")
    row_start, col_start = row_at * rows, lax.axis_index("col") * width
    copies[0].wait()
    copies[1].wait()
    masks = [block_fill(ref, row_start, col_start, rows, width) for ref in (fill_x_ref, fill_t_ref)]
    copies[2].wait()
    copies[3].wait()
    masked = [x_ref[...].astype(jnp.float32) * masks[0], t_ref[...].astype(jnp.float32) * masks[1]]
    pack(out_ref, masked, width)


def natural(block, rows, width, total):
    main, rem, lead = split(width)
    parts = [block[lead : lead + rows, k * main : (k + 1) * main] for k in range(total)]
    if rem:
        rems = unfold(block[:lead], rows, total * rem)
        parts = [
            jnp.concatenate([part, rems[:, k * rem : (k + 1) * rem]], axis=1)
            for k, part in enumerate(parts)
        ]
    return parts


def pack(out_ref, values, width):
    main, rem, lead = split(width)
    for k, value in enumerate(values):
        out_ref[0, lead:, k * main : (k + 1) * main] = value[:, :main].astype(out_ref.dtype)
    rows, lanes = values[0].shape[0], rem * len(values)
    for at in range(0, rows if rem else 0, FOLD):
        deep, left = min(FOLD, rows - at), at // FOLD * lanes
        for k, value in enumerate(values):
            part = value[at : at + deep, main:].astype(out_ref.dtype)
            out_ref[0, :deep, left + k * rem : left + (k + 1) * rem] = part


def mains_and_rems(block, rows, rem, lead, total):
    mains = block[lead:]
    return mains, (unfold(block[:lead], rows, total * rem) if rem else None)


def place(bits, position):
    offset = 0
    for at, weight in bits:
        offset = offset ^ (((position >> at) & 1) * weight)
    return offset


def walk(refs, step, carry):
    base = 0
    for ref in refs:
        count = ref.shape[0]
        if count <= 4:
            for i in range(count):
                carry = step(base + i, ref[i], carry)
        else:
            carry = lax.fori_loop(
                0, count, lambda i, c, ref=ref, base=base: step(base + i, ref[i], c), carry
            )
        base += count
    return carry


def panel_product(left, right, lhs, total, width, rows, places):
    row_bits, depth_bits, col_bits = places
    main, rem, lead = split(width)
    parts, top = width // rows, aligned(rows)
    my_row, my_depth, my_col = (lax.axis_index(a) for a in ("row", "depth", "col"))
    layers = lax.axis_size("depth")

    def fill(position, block, carry):
        col = my_col ^ place(col_bits, position)
        mains, rems = mains_and_rems(block, rows, rem, lead, total)
        for k in range(total):
            whole = mains[:, k * main : (k + 1) * main]
            if rem:
                whole = jnp.concatenate([whole, rems[:, k * rem : (k + 1) * rem]], axis=1)
            for h in range(parts):
                lhs[col * parts + h, k * top : k * top + rows, :] = whole[:, h * rows : (h + 1) * rows]
        return carry

    walk(left, fill, 0)

    def multiply(position, block, carry):
        row = my_row ^ place(row_bits, position)
        depth = my_depth ^ place(depth_bits, position)
        factor = lhs[row * layers + depth]
        operands = mains_and_rems(block, rows, rem, lead, 2)
        return tuple(
            c + jnp.dot(factor, o, preferred_element_type=jnp.float32)
            for c, o in zip(carry, operands[: len(carry)], strict=True)
        )

    sizes = (2 * main, 2 * rem) if rem else (2 * main,)
    zeros = tuple(jnp.zeros((lhs.shape[1], size), jnp.float32) for size in sizes)
    return walk(right, multiply, zeros)


def first_kernel(counts, places, width, *refs):
    n_left, n_right = counts
    left, right = refs[:n_left], refs[n_left : n_left + n_right]
    out_ref, lhs = refs[n_left + n_right :]
    main, rem, lead = split(width)
    rows = out_ref.shape[1] - lead
    top = aligned(rows)
    sums = panel_product(left, right, lhs, 2, width, rows, places)
    results = []
    for acc in sums:
        size = acc.shape[1] // 2
        square = acc[:rows, :size]
        cross = acc[top : top + rows, :size] + acc[:rows, size:]
        high = cross.astype(jnp.bfloat16).astype(jnp.float32)
        results.append((high, cross - high, square))
    for k, value in enumerate(results[0]):
        out_ref[0, lead:, k * main : (k + 1) * main] = value.astype(out_ref.dtype)
    if rem:
        folded = fold(jnp.concatenate(results[1], axis=1))
        out_ref[0, :FOLD, : folded.shape[1]] = folded.astype(out_ref.dtype)


def last_kernel(counts, places, width, *refs):
    n_left, n_right = counts
    left, right = refs[:n_left], refs[n_left : n_left + n_right]
    own_ref, out_ref, lhs = refs[n_left + n_right :]
    main, rem, lead = split(width)
    rows = out_ref.shape[0]
    top = aligned(rows)
    sums = panel_product(left, right, lhs, 3, width, rows, places)
    owns = mains_and_rems(own_ref[0], rows, rem, lead, 2)
    for acc, own, base in zip(sums, owns, (0, main)):
        size = acc.shape[1] // 2
        total = acc[:rows, :size] + acc[top : top + rows, :size] + acc[2 * top : 2 * top + rows, size:]
        out_ref[:, base : base + size] = 1.5 * own[:, size:].astype(jnp.float32) - 0.5 * total


def times(left, right):
    return jnp.dot(left, right, preferred_element_type=jnp.float32)


def add_panels(offsets, mine, others, lhs, rhs, width, rows):
    my_row, my_depth = lax.axis_index("row"), lax.axis_index("depth")
    top = aligned(rows)
    square = cross = jnp.zeros((rows, width), jnp.float32)
    for k, offset in enumerate(offsets):
        row = lax.rem(my_row + offset, lax.axis_size("row"))
        panels = []
        for a, b in zip(
            natural(mine[k], rows, width, 2), natural(others[k], rows, width, 2), strict=True
        ):
            a, b = a.astype(jnp.float32), b.astype(jnp.float32)
            halves = [jnp.where(my_depth == 0, a, b), jnp.where(my_depth == 0, b, a)]
            panels.append(jnp.concatenate(halves, axis=0).astype(jnp.bfloat16))
        for which, panel in enumerate(panels):
            rhs[row, which] = panel
        both = times(lhs[row], panels[0])
        square += both[:rows]
        cross += both[top : top + rows] + times(lhs[row, :rows], panels[1])
    return square, cross


def firsts_kernel(offsets, width, own, beside, *refs):
    mine, others = refs[: len(offsets)], refs[len(offsets) : 2 * len(offsets)]
    out_ref, low_ref, rhs, lhs = refs[2 * len(offsets) :]
    rows = own.shape[1] - split(width)[2]
    top = aligned(rows)
    my_col = lax.axis_index("col")
    for ref, across in ((own, 0), (beside, 1)):
        for k in range(2):
            col = my_col ^ across ^ (3 * k)
            for which, part in enumerate(natural(ref[k], rows, width, 2)):
                lhs[col, which * top : which * top + rows, :] = part
    square = cross = jnp.zeros((rows, width), jnp.float32)
    for row_offsets, left, right in zip(offsets, mine, others, strict=True):
        terms = add_panels(row_offsets, left, right, lhs, rhs, width, rows)
        square, cross = square + terms[0], cross + terms[1]
    high = cross.astype(jnp.bfloat16).astype(jnp.float32)
    pack(out_ref, (high, square), width)
    lead = split(width)[2]
    low_ref[...] = jnp.zeros_like(low_ref)
    low_ref[0, lead:, :width] = (cross - high).astype(low_ref.dtype)


def panel_terms(col, block, low, rhs, width, rows):
    main, rem, lead = split(width)
    total = times(block[lead : lead + rows, :main], rhs[col, 0, :main])
    total += times(block[lead : lead + rows, main : 2 * main], rhs[col, 1, :main])
    ends = jnp.concatenate([rhs[col, 0, main:], rhs[col, 1, main:]], axis=0)
    total += times(unfold(block[:lead], rows, 2 * rem), ends)
    if low is not None:
        total += times(low[lead:, :width], rhs[col, 0])
    return total


def near_lasts_kernel(width, mine, other, rhs, out_ref):
    rows = out_ref.shape[0]
    my_col = lax.axis_index("col")
    out_ref[...] = panel_terms(my_col, mine[0], mine[1], rhs, width, rows) + panel_terms(
        my_col ^ 1, other[0], other[1], rhs, width, rows
    )


def far_lasts_kernel(width, across, rhs, early, own_ref, out_ref):
    rows = out_ref.shape[0]
    my_col = lax.axis_index("col")
    total = early[...] + panel_terms(my_col ^ 3, across[0], None, rhs, width, rows)
    own = natural(own_ref[0], rows, width, 2)[1].astype(jnp.float32)
    out_ref[...] = 1.5 * own - 0.5 * total


def late_lasts_kernel(width, across, rhs, early, out_ref):
    rows = out_ref.shape[0]
    my_col = lax.axis_index("col")
    out_ref[...] = early[...] - 0.5 * panel_terms(my_col ^ 2, across[0], None, rhs, width, rows)


def call(kernel, name, out_shape, operands, scratch=(), **kwargs):
    return pl.pallas_call(
        kernel,
        out_shape=out_shape,
        in_specs=[VMEM] * len(operands),
        out_specs=jax.tree.map(lambda _: VMEM, out_shape),
        scratch_shapes=list(scratch),
        compiler_params=PARAMS,
        name=name,
        **kwargs,
    )(*operands)


def fast_body(block, rows, width):
    grid, top = lax.axis_size("row"), aligned(rows)
    shape = jax.ShapeDtypeStruct
    opposite = turn(block, "row", 2)
    line = jnp.concatenate([turn(block, "row", 1), turn(block, "row", 3), block], axis=0)
    side_line = swap(line, "depth", 1)
    side_opposite = swap(opposite, "depth", 1)
    held = jnp.concatenate([block, swap(block, "col", 3)], axis=0)
    beside = swap(held, "col", 1)
    panels = shape((grid, 2, width, width), jnp.bfloat16)
    firsts, low, rhs = call(
        functools.partial(firsts_kernel, ((1, 3, 0), (2,)), width),
        "firsts",
        (shape(block.shape, block.dtype), shape(block.shape, block.dtype), panels),
        (held, beside, line, opposite, side_line, side_opposite),
        [pltpu.VMEM((grid, 2 * top, width), jnp.bfloat16)],
    )
    across = swap(firsts, "col", 3)
    out = shape((rows, width), jnp.float32)
    mine = jnp.concatenate([firsts, low], axis=0)
    near = (mine, swap(mine, "col", 1))
    total = call(functools.partial(near_lasts_kernel, width), "near_lasts", out, (*near, rhs))
    total = call(functools.partial(far_lasts_kernel, width), "far_lasts", out, (across, rhs, total, block))
    return call(
        functools.partial(late_lasts_kernel, width),
        "late_lasts",
        out,
        (swap(across, "col", 1), rhs, total),
    )


def gather(block, axes):
    held, at, bits = block, 0, []
    for axis, steps in axes:
        meaning = []
        for step in steps:
            held = jnp.concatenate([held, swap(held, axis, step)], axis=0)
            meaning.append((at, step))
            at += 1
        bits.append(meaning)
    return [held], bits


def general_body(block, rows, width):
    def steps(axis):
        return [1 << k for k in range(lax.axis_size(axis).bit_length() - 1)]

    right, (row_bits, depth_bits) = gather(block, [(a, steps(a)) for a in ("row", "depth")])
    left, (col_bits,) = gather(block, [("col", steps("col")[::-1])])
    places = (row_bits, depth_bits, col_bits)
    blocks, top = right[0].shape[0], aligned(rows)
    _, _, lead = split(width)
    firsts = call(
        functools.partial(first_kernel, (1, 1), places, width),
        "firsts",
        jax.ShapeDtypeStruct((1, lead + rows, 3 * split(width)[0]), jnp.bfloat16),
        (*left, *right),
        [pltpu.VMEM((blocks, 2 * top, rows), jnp.bfloat16)],
    )
    left, (col_bits,) = gather(firsts, [("col", steps("col")[::-1])])
    return call(
        functools.partial(last_kernel, (1, 1), places, width),
        "lasts",
        jax.ShapeDtypeStruct((rows, width), jnp.float32),
        (*left, *right, block),
        [pltpu.VMEM((blocks, 3 * top, rows), jnp.bfloat16)],
    )


def body(x_matrix, tangent, fill_x, fill_t):
    rows, width = x_matrix.shape
    main, _, lead = split(width)
    block = pl.pallas_call(
        pack_kernel,
        out_shape=jax.ShapeDtypeStruct((1, lead + rows, 2 * main), jnp.bfloat16),
        in_specs=[HBM] * 4,
        out_specs=VMEM,
        scratch_shapes=[
            pltpu.VMEM((rows, width), jnp.bfloat16),
            pltpu.VMEM((rows, width), jnp.bfloat16),
            pltpu.SMEM(fill_x.shape, jnp.int32),
            pltpu.SMEM(fill_t.shape, jnp.int32),
            pltpu.SemaphoreType.DMA((4,)),
        ],
        compiler_params=PARAMS,
        name="pack",
    )(*(pltpu.with_memory_space_constraint(a, pltpu.HBM) for a in (x_matrix, tangent, fill_x, fill_t)))
    sizes = tuple(lax.axis_size(a) for a in ("row", "col", "depth"))
    return (fast_body if sizes == (4, 4, 2) else general_body)(block, rows, width)


def solution(mesh):
    placed = (P(("row", "depth"), "col"), P(("row", "depth"), "col"), P(), P())
    return jax.shard_map(
        body, mesh=mesh, in_specs=placed, out_specs=P(("row", "depth"), "col"), check_vma=False
    )
```

```python
import functools

import jax
import jax.numpy as jnp
from jax import lax
from jax.experimental import pallas as pl
from jax.experimental.pallas import tpu as pltpu
from jax.sharding import PartitionSpec as P

BLOCK = 128
LANES = 128
FOLD = 16
HBM = pl.BlockSpec(memory_space=pltpu.HBM)
VMEM = pl.BlockSpec(memory_space=pltpu.VMEM)
PARAMS = pltpu.CompilerParams(vmem_limit_bytes=48 * 1024 * 1024)


def aligned(rows):
    return -(-rows // 16) * 16


def split(width):
    rem = width % LANES
    return width - rem, rem, FOLD if rem else 0


def swap(value, axis, offset):
    size = lax.axis_size(axis)
    return lax.ppermute(value, axis, [(i, i ^ offset) for i in range(size)])


def turn(value, axis, offset):
    size = lax.axis_size(axis)
    return lax.ppermute(value, axis, [((i + offset) % size, i) for i in range(size)])


def block_fill(fill_ref, row_start, col_start, rows, width):
    count = fill_ref.shape[0]
    row_ids = row_start + lax.broadcasted_iota(jnp.int32, (rows, width), 0)
    col_ids = col_start + lax.broadcasted_iota(jnp.int32, (1, width), 1)
    first_row, first_col = row_start // BLOCK, col_start // BLOCK
    mask = None
    for i in range((rows - 2) // BLOCK + 2):
        row_at = jnp.minimum(first_row + i, count - 1)
        flags = None
        for j in range((width - 2) // BLOCK + 2):
            flag = fill_ref[row_at, jnp.minimum(first_col + j, count - 1)].astype(jnp.float32)
            passed = col_ids >= (first_col + j) * BLOCK
            flags = jnp.where(passed, flag, 0.0 if flags is None else flags)
        flags = jnp.broadcast_to(flags, (rows, width))
        mask = flags if mask is None else jnp.where(row_ids >= (first_row + i) * BLOCK, flags, mask)
    return mask


def fold(value):
    rows, lanes = value.shape
    spare = -rows % FOLD
    if spare:
        value = jnp.concatenate([value, jnp.zeros((spare, lanes), value.dtype)], axis=0)
    return jnp.concatenate([value[at : at + FOLD] for at in range(0, rows, FOLD)], axis=1)


def unfold(value, rows, lanes):
    groups = [value[:, k * lanes : (k + 1) * lanes] for k in range(-(-rows // FOLD))]
    return jnp.concatenate(groups, axis=0)[:rows]


def pack_kernel(
    x_hbm, t_hbm, fill_x_hbm, fill_t_hbm, out_ref, x_ref, t_ref, fill_x_ref, fill_t_ref, sems
):
    rows, width = x_ref.shape
    pairs = ((fill_x_hbm, fill_x_ref), (fill_t_hbm, fill_t_ref), (x_hbm, x_ref), (t_hbm, t_ref))
    copies = [pltpu.make_async_copy(src, dst, sems.at[k]) for k, (src, dst) in enumerate(pairs)]
    for copy in copies:
        copy.start()
    row_at = lax.axis_index("row") * lax.axis_size("depth") + lax.axis_index("depth")
    row_start, col_start = row_at * rows, lax.axis_index("col") * width
    copies[0].wait()
    copies[1].wait()
    masks = [block_fill(ref, row_start, col_start, rows, width) for ref in (fill_x_ref, fill_t_ref)]
    copies[2].wait()
    copies[3].wait()
    masked = [x_ref[...].astype(jnp.float32) * masks[0], t_ref[...].astype(jnp.float32) * masks[1]]
    pack(out_ref, masked, width)


def natural(block, rows, width, total):
    main, rem, lead = split(width)
    parts = [block[lead : lead + rows, k * main : (k + 1) * main] for k in range(total)]
    if rem:
        rems = unfold(block[:lead], rows, total * rem)
        parts = [
            jnp.concatenate([part, rems[:, k * rem : (k + 1) * rem]], axis=1)
            for k, part in enumerate(parts)
        ]
    return parts


def pack(out_ref, values, width):
    main, rem, lead = split(width)
    for k, value in enumerate(values):
        out_ref[0, lead:, k * main : (k + 1) * main] = value[:, :main].astype(out_ref.dtype)
    rows, lanes = values[0].shape[0], rem * len(values)
    for at in range(0, rows if rem else 0, FOLD):
        deep, left = min(FOLD, rows - at), at // FOLD * lanes
        for k, value in enumerate(values):
            part = value[at : at + deep, main:].astype(out_ref.dtype)
            out_ref[0, :deep, left + k * rem : left + (k + 1) * rem] = part


def mains_and_rems(block, rows, rem, lead, total):
    mains = block[lead:]
    return mains, (unfold(block[:lead], rows, total * rem) if rem else None)


def place(bits, position):
    offset = 0
    for at, weight in bits:
        offset = offset ^ (((position >> at) & 1) * weight)
    return offset


def walk(refs, step, carry):
    base = 0
    for ref in refs:
        count = ref.shape[0]
        if count <= 4:
            for i in range(count):
                carry = step(base + i, ref[i], carry)
        else:
            carry = lax.fori_loop(
                0, count, lambda i, c, ref=ref, base=base: step(base + i, ref[i], c), carry
            )
        base += count
    return carry


def panel_product(left, right, lhs, total, width, rows, places):
    row_bits, depth_bits, col_bits = places
    main, rem, lead = split(width)
    parts, top = width // rows, aligned(rows)
    my_row, my_depth, my_col = (lax.axis_index(a) for a in ("row", "depth", "col"))
    layers = lax.axis_size("depth")

    def fill(position, block, carry):
        col = my_col ^ place(col_bits, position)
        mains, rems = mains_and_rems(block, rows, rem, lead, total)
        for k in range(total):
            whole = mains[:, k * main : (k + 1) * main]
            if rem:
                whole = jnp.concatenate([whole, rems[:, k * rem : (k + 1) * rem]], axis=1)
            for h in range(parts):
                lhs[col * parts + h, k * top : k * top + rows, :] = whole[:, h * rows : (h + 1) * rows]
        return carry

    walk(left, fill, 0)

    def multiply(position, block, carry):
        row = my_row ^ place(row_bits, position)
        depth = my_depth ^ place(depth_bits, position)
        factor = lhs[row * layers + depth]
        operands = mains_and_rems(block, rows, rem, lead, 2)
        return tuple(
            c + jnp.dot(factor, o, preferred_element_type=jnp.float32)
            for c, o in zip(carry, operands[: len(carry)], strict=True)
        )

    sizes = (2 * main, 2 * rem) if rem else (2 * main,)
    zeros = tuple(jnp.zeros((lhs.shape[1], size), jnp.float32) for size in sizes)
    return walk(right, multiply, zeros)


def first_kernel(counts, places, width, *refs):
    n_left, n_right = counts
    left, right = refs[:n_left], refs[n_left : n_left + n_right]
    out_ref, lhs = refs[n_left + n_right :]
    main, rem, lead = split(width)
    rows = out_ref.shape[1] - lead
    top = aligned(rows)
    sums = panel_product(left, right, lhs, 2, width, rows, places)
    results = []
    for acc in sums:
        size = acc.shape[1] // 2
        square = acc[:rows, :size]
        cross = acc[top : top + rows, :size] + acc[:rows, size:]
        high = cross.astype(jnp.bfloat16).astype(jnp.float32)
        results.append((high, cross - high, square))
    for k, value in enumerate(results[0]):
        out_ref[0, lead:, k * main : (k + 1) * main] = value.astype(out_ref.dtype)
    if rem:
        folded = fold(jnp.concatenate(results[1], axis=1))
        out_ref[0, :FOLD, : folded.shape[1]] = folded.astype(out_ref.dtype)


def last_kernel(counts, places, width, *refs):
    n_left, n_right = counts
    left, right = refs[:n_left], refs[n_left : n_left + n_right]
    own_ref, out_ref, lhs = refs[n_left + n_right :]
    main, rem, lead = split(width)
    rows = out_ref.shape[0]
    top = aligned(rows)
    sums = panel_product(left, right, lhs, 3, width, rows, places)
    owns = mains_and_rems(own_ref[0], rows, rem, lead, 2)
    for acc, own, base in zip(sums, owns, (0, main)):
        size = acc.shape[1] // 2
        total = acc[:rows, :size] + acc[top : top + rows, :size] + acc[2 * top : 2 * top + rows, size:]
        out_ref[:, base : base + size] = 1.5 * own[:, size:].astype(jnp.float32) - 0.5 * total


def times(left, right):
    return jnp.dot(left, right, preferred_element_type=jnp.float32)


def add_panels(offsets, mine, others, lhs, rhs, width, rows):
    my_row, my_depth = lax.axis_index("row"), lax.axis_index("depth")
    top = aligned(rows)
    square = cross = jnp.zeros((rows, width), jnp.float32)
    for k, offset in enumerate(offsets):
        row = lax.rem(my_row + offset, lax.axis_size("row"))
        panels = []
        for a, b in zip(
            natural(mine[k], rows, width, 2), natural(others[k], rows, width, 2), strict=True
        ):
            a, b = a.astype(jnp.float32), b.astype(jnp.float32)
            halves = [jnp.where(my_depth == 0, a, b), jnp.where(my_depth == 0, b, a)]
            panels.append(jnp.concatenate(halves, axis=0).astype(jnp.bfloat16))
        for which, panel in enumerate(panels):
            rhs[row, which] = panel
        both = times(lhs[row], panels[0])
        square += both[:rows]
        cross += both[top : top + rows] + times(lhs[row, :rows], panels[1])
    return square, cross


def firsts_kernel(offsets, width, own, beside, *refs):
    mine, others = refs[: len(offsets)], refs[len(offsets) : 2 * len(offsets)]
    out_ref, low_ref, rhs, lhs = refs[2 * len(offsets) :]
    rows = own.shape[1] - split(width)[2]
    top = aligned(rows)
    my_col = lax.axis_index("col")
    for ref, across in ((own, 0), (beside, 1)):
        for k in range(2):
            col = my_col ^ across ^ (3 * k)
            for which, part in enumerate(natural(ref[k], rows, width, 2)):
                lhs[col, which * top : which * top + rows, :] = part
    square = cross = jnp.zeros((rows, width), jnp.float32)
    for row_offsets, left, right in zip(offsets, mine, others, strict=True):
        terms = add_panels(row_offsets, left, right, lhs, rhs, width, rows)
        square, cross = square + terms[0], cross + terms[1]
    high = cross.astype(jnp.bfloat16).astype(jnp.float32)
    pack(out_ref, (high, square), width)
    lead = split(width)[2]
    low_ref[...] = jnp.zeros_like(low_ref)
    low_ref[0, lead:, :width] = (cross - high).astype(low_ref.dtype)


def panel_terms(col, block, low, rhs, width, rows):
    main, rem, lead = split(width)
    total = times(block[lead : lead + rows, :main], rhs[col, 0, :main])
    total += times(block[lead : lead + rows, main : 2 * main], rhs[col, 1, :main])
    ends = jnp.concatenate([rhs[col, 0, main:], rhs[col, 1, main:]], axis=0)
    total += times(unfold(block[:lead], rows, 2 * rem), ends)
    if low is not None:
        total += times(low[lead:, :width], rhs[col, 0])
    return total


def far_lasts_kernel(offset, width, panel, rhs, own_ref, out_ref):
    rows = out_ref.shape[0]
    terms = panel_terms(lax.axis_index("col") ^ offset, panel[0], None, rhs, width, rows)
    own = natural(own_ref[0], rows, width, 2)[1].astype(jnp.float32)
    out_ref[...] = 1.5 * own - 0.5 * terms


def near_lasts_kernel(width, mine, other, rhs, early, out_ref):
    rows = out_ref.shape[0]
    my_col = lax.axis_index("col")
    terms = panel_terms(my_col, mine[0], mine[1], rhs, width, rows)
    terms += panel_terms(my_col ^ 1, other[0], other[1], rhs, width, rows)
    out_ref[...] = early[...] - 0.5 * terms


def late_lasts_kernel(offset, width, panel, rhs, early, out_ref):
    rows = out_ref.shape[0]
    terms = panel_terms(lax.axis_index("col") ^ offset, panel[0], None, rhs, width, rows)
    out_ref[...] = early[...] - 0.5 * terms


def call(kernel, name, out_shape, operands, scratch=(), **kwargs):
    return pl.pallas_call(
        kernel,
        out_shape=out_shape,
        in_specs=[VMEM] * len(operands),
        out_specs=jax.tree.map(lambda _: VMEM, out_shape),
        scratch_shapes=list(scratch),
        compiler_params=PARAMS,
        name=name,
        **kwargs,
    )(*operands)


def fast_body(block, rows, width):
    grid, top = lax.axis_size("row"), aligned(rows)
    shape = jax.ShapeDtypeStruct
    opposite = turn(block, "row", 2)
    line = jnp.concatenate([turn(block, "row", 1), turn(block, "row", 3), block], axis=0)
    side_line = swap(line, "depth", 1)
    side_opposite = swap(opposite, "depth", 1)
    held = jnp.concatenate([block, swap(block, "col", 3)], axis=0)
    beside = swap(held, "col", 1)
    panels = shape((grid, 2, width, width), jnp.bfloat16)
    firsts, low, rhs = call(
        functools.partial(firsts_kernel, ((1, 3, 0), (2,)), width),
        "firsts",
        (shape(block.shape, block.dtype), shape(block.shape, block.dtype), panels),
        (held, beside, line, opposite, side_line, side_opposite),
        [pltpu.VMEM((grid, 2 * top, width), jnp.bfloat16)],
    )
    out = shape((rows, width), jnp.float32)
    straight = swap(firsts, "col", 3)
    crossed = swap(firsts, "col", 2)
    mine = jnp.concatenate([firsts, low], axis=0)
    near = (mine, swap(mine, "col", 1))
    far = call(functools.partial(far_lasts_kernel, 3, width), "far_lasts", out, (straight, rhs, block), cost_estimate=pl.CostEstimate(flops=1000000000, bytes_accessed=0, transcendentals=0),)
    total = call(functools.partial(near_lasts_kernel, width), "near_lasts", out, (*near, rhs, far), )
    return call(
        functools.partial(late_lasts_kernel, 2, width), "late_lasts", out, (crossed, rhs, total)
    )


def gather(block, axes):
    held, at, bits = block, 0, []
    for axis, steps in axes:
        meaning = []
        for step in steps:
            held = jnp.concatenate([held, swap(held, axis, step)], axis=0)
            meaning.append((at, step))
            at += 1
        bits.append(meaning)
    return [held], bits


def general_body(block, rows, width):
    def steps(axis):
        return [1 << k for k in range(lax.axis_size(axis).bit_length() - 1)]

    right, (row_bits, depth_bits) = gather(block, [(a, steps(a)) for a in ("row", "depth")])
    left, (col_bits,) = gather(block, [("col", steps("col")[::-1])])
    places = (row_bits, depth_bits, col_bits)
    blocks, top = right[0].shape[0], aligned(rows)
    _, _, lead = split(width)
    firsts = call(
        functools.partial(first_kernel, (1, 1), places, width),
        "firsts",
        jax.ShapeDtypeStruct((1, lead + rows, 3 * split(width)[0]), jnp.bfloat16),
        (*left, *right),
        [pltpu.VMEM((blocks, 2 * top, rows), jnp.bfloat16)],
    )
    left, (col_bits,) = gather(firsts, [("col", steps("col")[::-1])])
    return call(
        functools.partial(last_kernel, (1, 1), places, width),
        "lasts",
        jax.ShapeDtypeStruct((rows, width), jnp.float32),
        (*left, *right, block),
        [pltpu.VMEM((blocks, 3 * top, rows), jnp.bfloat16)],
    )


def body(x_matrix, tangent, fill_x, fill_t):
    rows, width = x_matrix.shape
    main, _, lead = split(width)
    block = pl.pallas_call(
        pack_kernel,
        out_shape=jax.ShapeDtypeStruct((1, lead + rows, 2 * main), jnp.bfloat16),
        in_specs=[HBM] * 4,
        out_specs=VMEM,
        scratch_shapes=[
            pltpu.VMEM((rows, width), jnp.bfloat16),
            pltpu.VMEM((rows, width), jnp.bfloat16),
            pltpu.SMEM(fill_x.shape, jnp.int32),
            pltpu.SMEM(fill_t.shape, jnp.int32),
            pltpu.SemaphoreType.DMA((4,)),
        ],
        compiler_params=PARAMS,
        name="pack",
    )(*(pltpu.with_memory_space_constraint(a, pltpu.HBM) for a in (x_matrix, tangent, fill_x, fill_t)))
    sizes = tuple(lax.axis_size(a) for a in ("row", "col", "depth"))
    return (fast_body if sizes == (4, 4, 2) else general_body)(block, rows, width)


def solution(mesh):
    placed = (P(("row", "depth"), "col"), P(("row", "depth"), "col"), P(), P())
    return jax.shard_map(
        body, mesh=mesh, in_specs=placed, out_specs=P(("row", "depth"), "col"), check_vma=False
    )
```

```python
import functools

import jax
import jax.numpy as jnp
from jax import lax
from jax.experimental import pallas as pl
from jax.experimental.pallas import tpu as pltpu
from jax.sharding import PartitionSpec as P

BLOCK = 128
LANES = 128
FOLD = 16
TALL_FOLD = 24
HBM = pl.BlockSpec(memory_space=pltpu.HBM)
VMEM = pl.BlockSpec(memory_space=pltpu.VMEM)
PARAMS = pltpu.CompilerParams(vmem_limit_bytes=48 * 1024 * 1024)


def aligned(rows):
    return -(-rows // 16) * 16


def split(width):
    rem = width % LANES
    return width - rem, rem, FOLD if rem else 0


def swap(value, axis, offset):
    size = lax.axis_size(axis)
    return lax.ppermute(value, axis, [(i, i ^ offset) for i in range(size)])


def turn(value, axis, offset):
    size = lax.axis_size(axis)
    return lax.ppermute(value, axis, [((i + offset) % size, i) for i in range(size)])


def block_fill(fill_ref, row_start, col_start, rows, width):
    count = fill_ref.shape[0]
    row_ids = row_start + lax.broadcasted_iota(jnp.int32, (rows, width), 0)
    col_ids = col_start + lax.broadcasted_iota(jnp.int32, (1, width), 1)
    first_row, first_col = row_start // BLOCK, col_start // BLOCK
    mask = None
    for i in range((rows - 2) // BLOCK + 2):
        row_at = jnp.minimum(first_row + i, count - 1)
        flags = None
        for j in range((width - 2) // BLOCK + 2):
            flag = fill_ref[row_at, jnp.minimum(first_col + j, count - 1)].astype(jnp.float32)
            passed = col_ids >= (first_col + j) * BLOCK
            flags = jnp.where(passed, flag, 0.0 if flags is None else flags)
        flags = jnp.broadcast_to(flags, (rows, width))
        mask = flags if mask is None else jnp.where(row_ids >= (first_row + i) * BLOCK, flags, mask)
    return mask


def fold(value):
    rows, lanes = value.shape
    spare = -rows % FOLD
    if spare:
        value = jnp.concatenate([value, jnp.zeros((spare, lanes), value.dtype)], axis=0)
    return jnp.concatenate([value[at : at + FOLD] for at in range(0, rows, FOLD)], axis=1)


def unfold(value, rows, lanes, deep=FOLD):
    groups = [value[:, k * lanes : (k + 1) * lanes] for k in range(-(-rows // deep))]
    return jnp.concatenate(groups, axis=0)[:rows]


def pack_kernel(
    packer, x_hbm, t_hbm, fill_x_hbm, fill_t_hbm, out_ref, x_ref, t_ref, fill_x_ref, fill_t_ref, sems
):
    rows, width = x_ref.shape
    pairs = ((fill_x_hbm, fill_x_ref), (fill_t_hbm, fill_t_ref), (x_hbm, x_ref), (t_hbm, t_ref))
    copies = [pltpu.make_async_copy(src, dst, sems.at[k]) for k, (src, dst) in enumerate(pairs)]
    for copy in copies:
        copy.start()
    row_at = lax.axis_index("row") * lax.axis_size("depth") + lax.axis_index("depth")
    row_start, col_start = row_at * rows, lax.axis_index("col") * width
    copies[0].wait()
    copies[1].wait()
    masks = [block_fill(ref, row_start, col_start, rows, width) for ref in (fill_x_ref, fill_t_ref)]
    copies[2].wait()
    copies[3].wait()
    masked = [x_ref[...].astype(jnp.float32) * masks[0], t_ref[...].astype(jnp.float32) * masks[1]]
    packer(out_ref, masked, width)


def natural(block, rows, width, total):
    _, rem, _ = split(width)
    rems = unfold(block[:TALL_FOLD], rows, total * rem, TALL_FOLD)
    mains = [block[TALL_FOLD + k * rows : TALL_FOLD + (k + 1) * rows] for k in range(total)]
    return [
        jnp.concatenate([main, rems[:, k * rem : (k + 1) * rem]], axis=1)
        for k, main in enumerate(mains)
    ]


def tall_pack(out_ref, values, width):
    main, rem, _ = split(width)
    rows, lanes = values[0].shape[0], rem * len(values)
    for k, value in enumerate(values):
        top = TALL_FOLD + k * rows
        out_ref[0, top : top + rows, :] = value[:, :main].astype(out_ref.dtype)
        for at in range(0, rows, TALL_FOLD):
            deep, left = min(TALL_FOLD, rows - at), at // TALL_FOLD * lanes + k * rem
            part = value[at : at + deep, main:].astype(out_ref.dtype)
            out_ref[0, :deep, left : left + rem] = part


def pack(out_ref, values, width):
    main, rem, lead = split(width)
    for k, value in enumerate(values):
        out_ref[0, lead:, k * main : (k + 1) * main] = value[:, :main].astype(out_ref.dtype)
    rows, lanes = values[0].shape[0], rem * len(values)
    for at in range(0, rows if rem else 0, FOLD):
        deep, left = min(FOLD, rows - at), at // FOLD * lanes
        for k, value in enumerate(values):
            part = value[at : at + deep, main:].astype(out_ref.dtype)
            out_ref[0, :deep, left + k * rem : left + (k + 1) * rem] = part


def mains_and_rems(block, rows, rem, lead, total):
    mains = block[lead:]
    return mains, (unfold(block[:lead], rows, total * rem) if rem else None)


def place(bits, position):
    offset = 0
    for at, weight in bits:
        offset = offset ^ (((position >> at) & 1) * weight)
    return offset


def walk(refs, step, carry):
    base = 0
    for ref in refs:
        count = ref.shape[0]
        if count <= 4:
            for i in range(count):
                carry = step(base + i, ref[i], carry)
        else:
            carry = lax.fori_loop(
                0, count, lambda i, c, ref=ref, base=base: step(base + i, ref[i], c), carry
            )
        base += count
    return carry


def panel_product(left, right, lhs, total, width, rows, places):
    row_bits, depth_bits, col_bits = places
    main, rem, lead = split(width)
    parts, top = width // rows, aligned(rows)
    my_row, my_depth, my_col = (lax.axis_index(a) for a in ("row", "depth", "col"))
    layers = lax.axis_size("depth")

    def fill(position, block, carry):
        col = my_col ^ place(col_bits, position)
        mains, rems = mains_and_rems(block, rows, rem, lead, total)
        for k in range(total):
            whole = mains[:, k * main : (k + 1) * main]
            if rem:
                whole = jnp.concatenate([whole, rems[:, k * rem : (k + 1) * rem]], axis=1)
            for h in range(parts):
                lhs[col * parts + h, k * top : k * top + rows, :] = whole[:, h * rows : (h + 1) * rows]
        return carry

    walk(left, fill, 0)

    def multiply(position, block, carry):
        row = my_row ^ place(row_bits, position)
        depth = my_depth ^ place(depth_bits, position)
        factor = lhs[row * layers + depth]
        operands = mains_and_rems(block, rows, rem, lead, 2)
        return tuple(
            c + jnp.dot(factor, o, preferred_element_type=jnp.float32)
            for c, o in zip(carry, operands[: len(carry)], strict=True)
        )

    sizes = (2 * main, 2 * rem) if rem else (2 * main,)
    zeros = tuple(jnp.zeros((lhs.shape[1], size), jnp.float32) for size in sizes)
    return walk(right, multiply, zeros)


def first_kernel(counts, places, width, *refs):
    n_left, n_right = counts
    left, right = refs[:n_left], refs[n_left : n_left + n_right]
    out_ref, lhs = refs[n_left + n_right :]
    main, rem, lead = split(width)
    rows = out_ref.shape[1] - lead
    top = aligned(rows)
    sums = panel_product(left, right, lhs, 2, width, rows, places)
    results = []
    for acc in sums:
        size = acc.shape[1] // 2
        square = acc[:rows, :size]
        cross = acc[top : top + rows, :size] + acc[:rows, size:]
        high = cross.astype(jnp.bfloat16).astype(jnp.float32)
        results.append((high, cross - high, square))
    for k, value in enumerate(results[0]):
        out_ref[0, lead:, k * main : (k + 1) * main] = value.astype(out_ref.dtype)
    if rem:
        folded = fold(jnp.concatenate(results[1], axis=1))
        out_ref[0, :FOLD, : folded.shape[1]] = folded.astype(out_ref.dtype)


def last_kernel(counts, places, width, *refs):
    n_left, n_right = counts
    left, right = refs[:n_left], refs[n_left : n_left + n_right]
    own_ref, out_ref, lhs = refs[n_left + n_right :]
    main, rem, lead = split(width)
    rows = out_ref.shape[0]
    top = aligned(rows)
    sums = panel_product(left, right, lhs, 3, width, rows, places)
    owns = mains_and_rems(own_ref[0], rows, rem, lead, 2)
    for acc, own, base in zip(sums, owns, (0, main)):
        size = acc.shape[1] // 2
        total = acc[:rows, :size] + acc[top : top + rows, :size] + acc[2 * top : 2 * top + rows, size:]
        out_ref[:, base : base + size] = 1.5 * own[:, size:].astype(jnp.float32) - 0.5 * total


def times(left, right):
    return jnp.dot(left, right, preferred_element_type=jnp.float32)


def add_panels(offsets, mine, others, lhs, rhs, width, rows):
    my_row, my_depth = lax.axis_index("row"), lax.axis_index("depth")
    top = aligned(rows)
    square = cross = jnp.zeros((rows, width), jnp.float32)
    for k, offset in enumerate(offsets):
        row = lax.rem(my_row + offset, lax.axis_size("row"))
        panels = []
        for a, b in zip(
            natural(mine[k], rows, width, 2), natural(others[k], rows, width, 2), strict=True
        ):
            a, b = a.astype(jnp.float32), b.astype(jnp.float32)
            halves = [jnp.where(my_depth == 0, a, b), jnp.where(my_depth == 0, b, a)]
            panels.append(jnp.concatenate(halves, axis=0).astype(jnp.bfloat16))
        for which, panel in enumerate(panels):
            rhs[row, which] = panel
        both = times(lhs[row], panels[0])
        square += both[:rows]
        cross += both[top : top + rows] + times(lhs[row, :rows], panels[1])
    return square, cross


def firsts_kernel(offsets, width, own, beside, *refs):
    mine, others = refs[: len(offsets)], refs[len(offsets) : 2 * len(offsets)]
    out_ref, low_ref, rhs, lhs = refs[2 * len(offsets) :]
    rows = (own.shape[1] - TALL_FOLD) // 2
    top = aligned(rows)
    my_col = lax.axis_index("col")
    for ref, across in ((own, 0), (beside, 1)):
        for k in range(2):
            col = my_col ^ across ^ (3 * k)
            for which, part in enumerate(natural(ref[k], rows, width, 2)):
                lhs[col, which * top : which * top + rows, :] = part
    square = cross = jnp.zeros((rows, width), jnp.float32)
    for row_offsets, left, right in zip(offsets, mine, others, strict=True):
        terms = add_panels(row_offsets, left, right, lhs, rhs, width, rows)
        square, cross = square + terms[0], cross + terms[1]
    high = cross.astype(jnp.bfloat16).astype(jnp.float32)
    tall_pack(out_ref, (high, square), width)
    low = (cross - high).astype(low_ref.dtype)
    low_ref[...] = jnp.zeros_like(low_ref)
    low_ref[0, TALL_FOLD : TALL_FOLD + rows, :] = low[:, :LANES]
    low_ref[0, TALL_FOLD + rows :, : width - LANES] = low[:, LANES:]


def panel_terms(col, block, low, rhs, width, rows):
    main, rem, _ = split(width)
    first, second = TALL_FOLD, TALL_FOLD + rows
    total = times(block[first:second], rhs[col, 0, :main])
    total += times(block[second:], rhs[col, 1, :main])
    ends = jnp.concatenate([rhs[col, 0, main:], rhs[col, 1, main:]], axis=0)
    total += times(unfold(block[:first], rows, 2 * rem, TALL_FOLD), ends)
    if low is not None:
        total += times(low[first:second], rhs[col, 0, :main])
        total += times(low[second:, :rem], rhs[col, 0, main:])
    return total


def far_lasts_kernel(offset, width, panel, rhs, own_ref, out_ref):
    rows = out_ref.shape[0]
    terms = panel_terms(lax.axis_index("col") ^ offset, panel[0], None, rhs, width, rows)
    own = natural(own_ref[0], rows, width, 2)[1].astype(jnp.float32)
    out_ref[...] = 1.5 * own - 0.5 * terms


def near_lasts_kernel(width, mine, other, rhs, early, out_ref):
    rows = out_ref.shape[0]
    my_col = lax.axis_index("col")
    terms = panel_terms(my_col, mine[0], mine[1], rhs, width, rows)
    terms += panel_terms(my_col ^ 1, other[0], other[1], rhs, width, rows)
    out_ref[...] = early[...] - 0.5 * terms


def late_lasts_kernel(offset, width, panel, rhs, early, out_ref):
    rows = out_ref.shape[0]
    terms = panel_terms(lax.axis_index("col") ^ offset, panel[0], None, rhs, width, rows)
    out_ref[...] = early[...] - 0.5 * terms


def call(kernel, name, out_shape, operands, scratch=(), **kwargs):
    return pl.pallas_call(
        kernel,
        out_shape=out_shape,
        in_specs=[VMEM] * len(operands),
        out_specs=jax.tree.map(lambda _: VMEM, out_shape),
        scratch_shapes=list(scratch),
        compiler_params=PARAMS,
        name=name,
        **kwargs,
    )(*operands)


def fast_body(block, rows, width):
    grid, top = lax.axis_size("row"), aligned(rows)
    shape = jax.ShapeDtypeStruct
    opposite = turn(block, "row", 2)
    line = jnp.concatenate([turn(block, "row", 1), turn(block, "row", 3), block], axis=0)
    side_line = swap(line, "depth", 1)
    side_opposite = swap(opposite, "depth", 1)
    held = jnp.concatenate([block, swap(block, "col", 3)], axis=0)
    beside = swap(held, "col", 1)
    panels = shape((grid, 2, width, width), jnp.bfloat16)
    firsts, low, rhs = call(
        functools.partial(firsts_kernel, ((1, 3, 0), (2,)), width),
        "firsts",
        (shape(block.shape, block.dtype), shape(block.shape, block.dtype), panels),
        (held, beside, line, opposite, side_line, side_opposite),
        [pltpu.VMEM((grid, 2 * top, width), jnp.bfloat16)],
    )
    out = shape((rows, width), jnp.float32)
    straight = swap(firsts, "col", 3)
    crossed = swap(firsts, "col", 2)
    mine = jnp.concatenate([firsts, low], axis=0)
    near = (mine, swap(mine, "col", 1))
    far = call(functools.partial(far_lasts_kernel, 3, width), "far_lasts", out, (straight, rhs, block), cost_estimate=pl.CostEstimate(flops=1000000000, bytes_accessed=0, transcendentals=0),)
    total = call(functools.partial(near_lasts_kernel, width), "near_lasts", out, (*near, rhs, far), )
    return call(
        functools.partial(late_lasts_kernel, 2, width), "late_lasts", out, (crossed, rhs, total)
    )


def gather(block, axes):
    held, at, bits = block, 0, []
    for axis, steps in axes:
        meaning = []
        for step in steps:
            held = jnp.concatenate([held, swap(held, axis, step)], axis=0)
            meaning.append((at, step))
            at += 1
        bits.append(meaning)
    return [held], bits


def general_body(block, rows, width):
    def steps(axis):
        return [1 << k for k in range(lax.axis_size(axis).bit_length() - 1)]

    right, (row_bits, depth_bits) = gather(block, [(a, steps(a)) for a in ("row", "depth")])
    left, (col_bits,) = gather(block, [("col", steps("col")[::-1])])
    places = (row_bits, depth_bits, col_bits)
    blocks, top = right[0].shape[0], aligned(rows)
    _, _, lead = split(width)
    firsts = call(
        functools.partial(first_kernel, (1, 1), places, width),
        "firsts",
        jax.ShapeDtypeStruct((1, lead + rows, 3 * split(width)[0]), jnp.bfloat16),
        (*left, *right),
        [pltpu.VMEM((blocks, 2 * top, rows), jnp.bfloat16)],
    )
    left, (col_bits,) = gather(firsts, [("col", steps("col")[::-1])])
    return call(
        functools.partial(last_kernel, (1, 1), places, width),
        "lasts",
        jax.ShapeDtypeStruct((rows, width), jnp.float32),
        (*left, *right, block),
        [pltpu.VMEM((blocks, 3 * top, rows), jnp.bfloat16)],
    )


def body(x_matrix, tangent, fill_x, fill_t):
    rows, width = x_matrix.shape
    sizes = tuple(lax.axis_size(a) for a in ("row", "col", "depth"))
    main, rem, lead = split(width)
    fast = sizes == (4, 4, 2) and main == LANES and rem > 0 and rows % TALL_FOLD == 0
    fast = fast and 2 * rem * (rows // TALL_FOLD) <= LANES
    packed = (TALL_FOLD + 2 * rows, LANES) if fast else (lead + rows, 2 * main)
    block = pl.pallas_call(
        functools.partial(pack_kernel, tall_pack if fast else pack),
        out_shape=jax.ShapeDtypeStruct((1, *packed), jnp.bfloat16),
        in_specs=[HBM] * 4,
        out_specs=VMEM,
        scratch_shapes=[
            pltpu.VMEM((rows, width), jnp.bfloat16),
            pltpu.VMEM((rows, width), jnp.bfloat16),
            pltpu.SMEM(fill_x.shape, jnp.int32),
            pltpu.SMEM(fill_t.shape, jnp.int32),
            pltpu.SemaphoreType.DMA((4,)),
        ],
        compiler_params=PARAMS,
        name="pack",
    )(*(pltpu.with_memory_space_constraint(a, pltpu.HBM) for a in (x_matrix, tangent, fill_x, fill_t)))
    return (fast_body if fast else general_body)(block, rows, width)


def solution(mesh):
    placed = (P(("row", "depth"), "col"), P(("row", "depth"), "col"), P(), P())
    return jax.shard_map(
        body, mesh=mesh, in_specs=placed, out_specs=P(("row", "depth"), "col"), check_vma=False
    )
```

```python
import functools

import jax
import jax.numpy as jnp
from jax import lax
from jax.experimental import pallas as pl
from jax.experimental.pallas import tpu as pltpu
from jax.sharding import PartitionSpec as P

BLOCK = 128
LANES = 128
FOLD = 16
TALL_FOLD = 24
HBM = pl.BlockSpec(memory_space=pltpu.HBM)
VMEM = pl.BlockSpec(memory_space=pltpu.VMEM)
PARAMS = pltpu.CompilerParams(vmem_limit_bytes=48 * 1024 * 1024)


def aligned(rows):
    return -(-rows // 16) * 16


def split(width):
    rem = width % LANES
    return width - rem, rem, FOLD if rem else 0


def swap(value, axis, offset):
    size = lax.axis_size(axis)
    return lax.ppermute(value, axis, [(i, i ^ offset) for i in range(size)])


def turn(value, axis, offset):
    size = lax.axis_size(axis)
    return lax.ppermute(value, axis, [((i + offset) % size, i) for i in range(size)])


def block_fill(fill_ref, row_start, col_start, rows, width):
    count = fill_ref.shape[0]
    row_ids = row_start + lax.broadcasted_iota(jnp.int32, (rows, width), 0)
    col_ids = col_start + lax.broadcasted_iota(jnp.int32, (1, width), 1)
    first_row, first_col = row_start // BLOCK, col_start // BLOCK
    mask = None
    for i in range((rows - 2) // BLOCK + 2):
        row_at = jnp.minimum(first_row + i, count - 1)
        flags = None
        for j in range((width - 2) // BLOCK + 2):
            flag = fill_ref[row_at, jnp.minimum(first_col + j, count - 1)].astype(jnp.float32)
            passed = col_ids >= (first_col + j) * BLOCK
            flags = jnp.where(passed, flag, 0.0 if flags is None else flags)
        flags = jnp.broadcast_to(flags, (rows, width))
        mask = flags if mask is None else jnp.where(row_ids >= (first_row + i) * BLOCK, flags, mask)
    return mask


def fold(value):
    rows, lanes = value.shape
    spare = -rows % FOLD
    if spare:
        value = jnp.concatenate([value, jnp.zeros((spare, lanes), value.dtype)], axis=0)
    return jnp.concatenate([value[at : at + FOLD] for at in range(0, rows, FOLD)], axis=1)


def unfold(value, rows, lanes, deep=FOLD):
    groups = [value[:, k * lanes : (k + 1) * lanes] for k in range(-(-rows // deep))]
    return jnp.concatenate(groups, axis=0)[:rows]


def pack_kernel(
    packer, x_hbm, t_hbm, fill_x_hbm, fill_t_hbm, out_ref, x_ref, t_ref, fill_x_ref, fill_t_ref, sems
):
    rows, width = x_ref.shape
    pairs = ((fill_x_hbm, fill_x_ref), (fill_t_hbm, fill_t_ref), (x_hbm, x_ref), (t_hbm, t_ref))
    copies = [pltpu.make_async_copy(src, dst, sems.at[k]) for k, (src, dst) in enumerate(pairs)]
    for copy in copies:
        copy.start()
    row_at = lax.axis_index("row") * lax.axis_size("depth") + lax.axis_index("depth")
    row_start, col_start = row_at * rows, lax.axis_index("col") * width
    copies[0].wait()
    copies[1].wait()
    masks = [block_fill(ref, row_start, col_start, rows, width) for ref in (fill_x_ref, fill_t_ref)]
    copies[2].wait()
    copies[3].wait()
    masked = [x_ref[...].astype(jnp.float32) * masks[0], t_ref[...].astype(jnp.float32) * masks[1]]
    packer(out_ref, masked, width)


def natural(block, rows, width, total):
    _, rem, _ = split(width)
    rems = unfold(block[:TALL_FOLD], rows, total * rem, TALL_FOLD)
    mains = [block[TALL_FOLD + k * rows : TALL_FOLD + (k + 1) * rows] for k in range(total)]
    return [
        jnp.concatenate([main, rems[:, k * rem : (k + 1) * rem]], axis=1)
        for k, main in enumerate(mains)
    ]


def tall_pack(out_ref, values, width):
    main, rem, _ = split(width)
    rows, lanes = values[0].shape[0], rem * len(values)
    for k, value in enumerate(values):
        top = TALL_FOLD + k * rows
        out_ref[0, top : top + rows, :] = value[:, :main].astype(out_ref.dtype)
        for at in range(0, rows, TALL_FOLD):
            deep, left = min(TALL_FOLD, rows - at), at // TALL_FOLD * lanes + k * rem
            part = value[at : at + deep, main:].astype(out_ref.dtype)
            out_ref[0, :deep, left : left + rem] = part


def pack(out_ref, values, width):
    main, rem, lead = split(width)
    for k, value in enumerate(values):
        out_ref[0, lead:, k * main : (k + 1) * main] = value[:, :main].astype(out_ref.dtype)
    rows, lanes = values[0].shape[0], rem * len(values)
    for at in range(0, rows if rem else 0, FOLD):
        deep, left = min(FOLD, rows - at), at // FOLD * lanes
        for k, value in enumerate(values):
            part = value[at : at + deep, main:].astype(out_ref.dtype)
            out_ref[0, :deep, left + k * rem : left + (k + 1) * rem] = part


def mains_and_rems(block, rows, rem, lead, total):
    mains = block[lead:]
    return mains, (unfold(block[:lead], rows, total * rem) if rem else None)


def place(bits, position):
    offset = 0
    for at, weight in bits:
        offset = offset ^ (((position >> at) & 1) * weight)
    return offset


def walk(refs, step, carry):
    base = 0
    for ref in refs:
        count = ref.shape[0]
        if count <= 4:
            for i in range(count):
                carry = step(base + i, ref[i], carry)
        else:
            carry = lax.fori_loop(
                0, count, lambda i, c, ref=ref, base=base: step(base + i, ref[i], c), carry
            )
        base += count
    return carry


def panel_product(left, right, lhs, total, width, rows, places):
    row_bits, depth_bits, col_bits = places
    main, rem, lead = split(width)
    parts, top = width // rows, aligned(rows)
    my_row, my_depth, my_col = (lax.axis_index(a) for a in ("row", "depth", "col"))
    layers = lax.axis_size("depth")

    def fill(position, block, carry):
        col = my_col ^ place(col_bits, position)
        mains, rems = mains_and_rems(block, rows, rem, lead, total)
        for k in range(total):
            whole = mains[:, k * main : (k + 1) * main]
            if rem:
                whole = jnp.concatenate([whole, rems[:, k * rem : (k + 1) * rem]], axis=1)
            for h in range(parts):
                lhs[col * parts + h, k * top : k * top + rows, :] = whole[:, h * rows : (h + 1) * rows]
        return carry

    walk(left, fill, 0)

    def multiply(position, block, carry):
        row = my_row ^ place(row_bits, position)
        depth = my_depth ^ place(depth_bits, position)
        factor = lhs[row * layers + depth]
        operands = mains_and_rems(block, rows, rem, lead, 2)
        return tuple(
            c + jnp.dot(factor, o, preferred_element_type=jnp.float32)
            for c, o in zip(carry, operands[: len(carry)], strict=True)
        )

    sizes = (2 * main, 2 * rem) if rem else (2 * main,)
    zeros = tuple(jnp.zeros((lhs.shape[1], size), jnp.float32) for size in sizes)
    return walk(right, multiply, zeros)


def first_kernel(counts, places, width, *refs):
    n_left, n_right = counts
    left, right = refs[:n_left], refs[n_left : n_left + n_right]
    out_ref, lhs = refs[n_left + n_right :]
    main, rem, lead = split(width)
    rows = out_ref.shape[1] - lead
    top = aligned(rows)
    sums = panel_product(left, right, lhs, 2, width, rows, places)
    results = []
    for acc in sums:
        size = acc.shape[1] // 2
        square = acc[:rows, :size]
        cross = acc[top : top + rows, :size] + acc[:rows, size:]
        high = cross.astype(jnp.bfloat16).astype(jnp.float32)
        results.append((high, cross - high, square))
    for k, value in enumerate(results[0]):
        out_ref[0, lead:, k * main : (k + 1) * main] = value.astype(out_ref.dtype)
    if rem:
        folded = fold(jnp.concatenate(results[1], axis=1))
        out_ref[0, :FOLD, : folded.shape[1]] = folded.astype(out_ref.dtype)


def last_kernel(counts, places, width, *refs):
    n_left, n_right = counts
    left, right = refs[:n_left], refs[n_left : n_left + n_right]
    own_ref, out_ref, lhs = refs[n_left + n_right :]
    main, rem, lead = split(width)
    rows = out_ref.shape[0]
    top = aligned(rows)
    sums = panel_product(left, right, lhs, 3, width, rows, places)
    owns = mains_and_rems(own_ref[0], rows, rem, lead, 2)
    for acc, own, base in zip(sums, owns, (0, main)):
        size = acc.shape[1] // 2
        total = acc[:rows, :size] + acc[top : top + rows, :size] + acc[2 * top : 2 * top + rows, size:]
        out_ref[:, base : base + size] = 1.5 * own[:, size:].astype(jnp.float32) - 0.5 * total


def times(left, right):
    return jnp.dot(left, right, preferred_element_type=jnp.float32)


def add_panels(offsets, mine, others, lhs, rhs, width, rows):
    my_row, my_depth = lax.axis_index("row"), lax.axis_index("depth")
    top = aligned(rows)
    square = cross = jnp.zeros((rows, width), jnp.float32)
    for k, offset in enumerate(offsets):
        row = lax.rem(my_row + offset, lax.axis_size("row"))
        panels = []
        for a, b in zip(
            natural(mine[k], rows, width, 2), natural(others[k], rows, width, 2), strict=True
        ):
            a, b = a.astype(jnp.float32), b.astype(jnp.float32)
            halves = [jnp.where(my_depth == 0, a, b), jnp.where(my_depth == 0, b, a)]
            panels.append(jnp.concatenate(halves, axis=0).astype(jnp.bfloat16))
        for which, panel in enumerate(panels):
            rhs[row, which] = panel
        both = times(lhs[row], panels[0])
        square += both[:rows]
        cross += both[top : top + rows] + times(lhs[row, :rows], panels[1])
    return square, cross


def firsts_kernel(offsets, width, own, beside, *refs):
    mine, others = refs[: len(offsets)], refs[len(offsets) : 2 * len(offsets)]
    out_ref, low_ref, rhs, lhs = refs[2 * len(offsets) :]
    rows = (own.shape[1] - TALL_FOLD) // 2
    top = aligned(rows)
    my_col = lax.axis_index("col")
    for ref, across in ((own, 0), (beside, 1)):
        for k in range(2):
            col = my_col ^ across ^ (3 * k)
            for which, part in enumerate(natural(ref[k], rows, width, 2)):
                lhs[col, which * top : which * top + rows, :] = part
    square = cross = jnp.zeros((rows, width), jnp.float32)
    for row_offsets, left, right in zip(offsets, mine, others, strict=True):
        terms = add_panels(row_offsets, left, right, lhs, rhs, width, rows)
        square, cross = square + terms[0], cross + terms[1]
    high = cross.astype(jnp.bfloat16).astype(jnp.float32)
    tall_pack(out_ref, (high, square), width)
    low = (cross - high).astype(low_ref.dtype)
    low_ref[...] = jnp.zeros_like(low_ref)
    low_ref[0, TALL_FOLD : TALL_FOLD + rows, :] = low[:, :LANES]
    low_ref[0, TALL_FOLD + rows :, : width - LANES] = low[:, LANES:]


def panel_terms(col, block, low, rhs, width, rows):
    main, rem, _ = split(width)
    first, second = TALL_FOLD, TALL_FOLD + rows
    total = times(block[first:second], rhs[col, 0, :main])
    total += times(block[second:], rhs[col, 1, :main])
    ends = jnp.concatenate([rhs[col, 0, main:], rhs[col, 1, main:]], axis=0)
    total += times(unfold(block[:first], rows, 2 * rem, TALL_FOLD), ends)
    if low is not None:
        total += times(low[first:second], rhs[col, 0, :main])
        total += times(low[second:, :rem], rhs[col, 0, main:])
    return total


def far_lasts_kernel(offset, width, panel, rhs, own_ref, out_ref):
    rows = out_ref.shape[0]
    terms = panel_terms(lax.axis_index("col") ^ offset, panel[0], None, rhs, width, rows)
    own = natural(own_ref[0], rows, width, 2)[1].astype(jnp.float32)
    out_ref[...] = 1.5 * own - 0.5 * terms


def near_lasts_kernel(width, mine, other, rhs, early, out_ref, ends_ref):
    rows = out_ref.shape[0]
    my_col = lax.axis_index("col")
    terms = panel_terms(my_col, mine[0], mine[1], rhs, width, rows)
    terms += panel_terms(my_col ^ 1, other[0], other[1], rhs, width, rows)
    out_ref[...] = early[...] - 0.5 * terms
    main, rem, _ = split(width)
    col = my_col ^ 2
    ends_ref[...] = jnp.zeros_like(ends_ref)
    for group in range(ends_ref.shape[0]):
        for which in range(2):
            at = (2 * group + which) * rem
            ends_ref[group, at : at + rem] = rhs[col, which, main:]


def late_lasts_kernel(offset, width, panel, rhs, early, ends, out_ref):
    rows, main = out_ref.shape[0], split(width)[0]
    col = lax.axis_index("col") ^ offset
    first, second = TALL_FOLD, TALL_FOLD + rows
    terms = times(panel[0, first:second], rhs[col, 0, :main])
    terms += times(panel[0, second:], rhs[col, 1, :main])
    folded = panel[0, :first, : ends.shape[1]]
    groups = [times(folded, ends[group]) for group in range(ends.shape[0])]
    out_ref[...] = early[...] - 0.5 * (terms + jnp.concatenate(groups, axis=0))


def call(kernel, name, out_shape, operands, scratch=(), **kwargs):
    return pl.pallas_call(
        kernel,
        out_shape=out_shape,
        in_specs=[VMEM] * len(operands),
        out_specs=jax.tree.map(lambda _: VMEM, out_shape),
        scratch_shapes=list(scratch),
        compiler_params=PARAMS,
        name=name,
        **kwargs,
    )(*operands)


def fast_body(block, rows, width):
    grid, top = lax.axis_size("row"), aligned(rows)
    shape = jax.ShapeDtypeStruct
    opposite = turn(block, "row", 2)
    line = jnp.concatenate([turn(block, "row", 1), turn(block, "row", 3), block], axis=0)
    side_line = swap(line, "depth", 1)
    side_opposite = swap(opposite, "depth", 1)
    held = jnp.concatenate([block, swap(block, "col", 3)], axis=0)
    beside = swap(held, "col", 1)
    panels = shape((grid, 2, width, width), jnp.bfloat16)
    firsts, low, rhs = call(
        functools.partial(firsts_kernel, ((1, 3, 0), (2,)), width),
        "firsts",
        (shape(block.shape, block.dtype), shape(block.shape, block.dtype), panels),
        (held, beside, line, opposite, side_line, side_opposite),
        [pltpu.VMEM((grid, 2 * top, width), jnp.bfloat16)],
    )
    out = shape((rows, width), jnp.float32)
    straight = swap(firsts, "col", 3)
    crossed = swap(firsts, "col", 2)
    mine = jnp.concatenate([firsts, low], axis=0)
    near = (mine, swap(mine, "col", 1))
    far = call(functools.partial(far_lasts_kernel, 3, width), "far_lasts", out, (straight, rhs, block), cost_estimate=pl.CostEstimate(flops=1000000000, bytes_accessed=0, transcendentals=0),)
    rem, groups = split(width)[1], rows // TALL_FOLD
    ends = shape((groups, groups * 2 * rem, width), block.dtype)
    total, ends = call(
        functools.partial(near_lasts_kernel, width), "near_lasts", (out, ends), (*near, rhs, far)
    )
    return call(
        functools.partial(late_lasts_kernel, 2, width), "late_lasts", out, (crossed, rhs, total, ends)
    )


def gather(block, axes):
    held, at, bits = block, 0, []
    for axis, steps in axes:
        meaning = []
        for step in steps:
            held = jnp.concatenate([held, swap(held, axis, step)], axis=0)
            meaning.append((at, step))
            at += 1
        bits.append(meaning)
    return [held], bits


def general_body(block, rows, width):
    def steps(axis):
        return [1 << k for k in range(lax.axis_size(axis).bit_length() - 1)]

    right, (row_bits, depth_bits) = gather(block, [(a, steps(a)) for a in ("row", "depth")])
    left, (col_bits,) = gather(block, [("col", steps("col")[::-1])])
    places = (row_bits, depth_bits, col_bits)
    blocks, top = right[0].shape[0], aligned(rows)
    _, _, lead = split(width)
    firsts = call(
        functools.partial(first_kernel, (1, 1), places, width),
        "firsts",
        jax.ShapeDtypeStruct((1, lead + rows, 3 * split(width)[0]), jnp.bfloat16),
        (*left, *right),
        [pltpu.VMEM((blocks, 2 * top, rows), jnp.bfloat16)],
    )
    left, (col_bits,) = gather(firsts, [("col", steps("col")[::-1])])
    return call(
        functools.partial(last_kernel, (1, 1), places, width),
        "lasts",
        jax.ShapeDtypeStruct((rows, width), jnp.float32),
        (*left, *right, block),
        [pltpu.VMEM((blocks, 3 * top, rows), jnp.bfloat16)],
    )


def body(x_matrix, tangent, fill_x, fill_t):
    rows, width = x_matrix.shape
    sizes = tuple(lax.axis_size(a) for a in ("row", "col", "depth"))
    main, rem, lead = split(width)
    fast = sizes == (4, 4, 2) and main == LANES and rem > 0 and rows % TALL_FOLD == 0
    fast = fast and 2 * rem * (rows // TALL_FOLD) <= LANES
    packed = (TALL_FOLD + 2 * rows, LANES) if fast else (lead + rows, 2 * main)
    block = pl.pallas_call(
        functools.partial(pack_kernel, tall_pack if fast else pack),
        out_shape=jax.ShapeDtypeStruct((1, *packed), jnp.bfloat16),
        in_specs=[HBM] * 4,
        out_specs=VMEM,
        scratch_shapes=[
            pltpu.VMEM((rows, width), jnp.bfloat16),
            pltpu.VMEM((rows, width), jnp.bfloat16),
            pltpu.SMEM(fill_x.shape, jnp.int32),
            pltpu.SMEM(fill_t.shape, jnp.int32),
            pltpu.SemaphoreType.DMA((4,)),
        ],
        compiler_params=PARAMS,
        name="pack",
    )(*(pltpu.with_memory_space_constraint(a, pltpu.HBM) for a in (x_matrix, tangent, fill_x, fill_t)))
    return (fast_body if fast else general_body)(block, rows, width)


def solution(mesh):
    placed = (P(("row", "depth"), "col"), P(("row", "depth"), "col"), P(), P())
    return jax.shard_map(
        body, mesh=mesh, in_specs=placed, out_specs=P(("row", "depth"), "col"), check_vma=False
    )
```

```python
import functools

import jax
import jax.numpy as jnp
from jax import lax
from jax.experimental import pallas as pl
from jax.experimental.pallas import tpu as pltpu
from jax.sharding import PartitionSpec as P

BLOCK = 128
LANES = 128
FOLD = 16
TALL_FOLD = 24
HBM = pl.BlockSpec(memory_space=pltpu.HBM)
VMEM = pl.BlockSpec(memory_space=pltpu.VMEM)
PARAMS = pltpu.CompilerParams(vmem_limit_bytes=48 * 1024 * 1024)


def aligned(rows):
    return -(-rows // 16) * 16


def split(width):
    rem = width % LANES
    return width - rem, rem, FOLD if rem else 0


def swap(value, axis, offset):
    size = lax.axis_size(axis)
    return lax.ppermute(value, axis, [(i, i ^ offset) for i in range(size)])


def turn(value, axis, offset):
    size = lax.axis_size(axis)
    return lax.ppermute(value, axis, [((i + offset) % size, i) for i in range(size)])


def block_fill(fill_ref, row_start, col_start, rows, width):
    count = fill_ref.shape[0]
    row_ids = row_start + lax.broadcasted_iota(jnp.int32, (rows, width), 0)
    col_ids = col_start + lax.broadcasted_iota(jnp.int32, (1, width), 1)
    first_row, first_col = row_start // BLOCK, col_start // BLOCK
    mask = None
    for i in range((rows - 2) // BLOCK + 2):
        row_at = jnp.minimum(first_row + i, count - 1)
        flags = None
        for j in range((width - 2) // BLOCK + 2):
            flag = fill_ref[row_at, jnp.minimum(first_col + j, count - 1)].astype(jnp.float32)
            passed = col_ids >= (first_col + j) * BLOCK
            flags = jnp.where(passed, flag, 0.0 if flags is None else flags)
        flags = jnp.broadcast_to(flags, (rows, width))
        mask = flags if mask is None else jnp.where(row_ids >= (first_row + i) * BLOCK, flags, mask)
    return mask


def fold(value):
    rows, lanes = value.shape
    spare = -rows % FOLD
    if spare:
        value = jnp.concatenate([value, jnp.zeros((spare, lanes), value.dtype)], axis=0)
    return jnp.concatenate([value[at : at + FOLD] for at in range(0, rows, FOLD)], axis=1)


def unfold(value, rows, lanes, deep=FOLD):
    groups = [value[:, k * lanes : (k + 1) * lanes] for k in range(-(-rows // deep))]
    return jnp.concatenate(groups, axis=0)[:rows]


def pack_kernel(
    packer, x_hbm, t_hbm, fill_x_hbm, fill_t_hbm, out_ref, x_ref, t_ref, fill_x_ref, fill_t_ref, sems
):
    rows, width = x_ref.shape
    pairs = ((fill_x_hbm, fill_x_ref), (fill_t_hbm, fill_t_ref), (x_hbm, x_ref), (t_hbm, t_ref))
    copies = [pltpu.make_async_copy(src, dst, sems.at[k]) for k, (src, dst) in enumerate(pairs)]
    for copy in copies:
        copy.start()
    row_at = lax.axis_index("row") * lax.axis_size("depth") + lax.axis_index("depth")
    row_start, col_start = row_at * rows, lax.axis_index("col") * width
    copies[0].wait()
    copies[1].wait()
    masks = [block_fill(ref, row_start, col_start, rows, width) for ref in (fill_x_ref, fill_t_ref)]
    copies[2].wait()
    copies[3].wait()
    masked = [x_ref[...].astype(jnp.float32) * masks[0], t_ref[...].astype(jnp.float32) * masks[1]]
    packer(out_ref, masked, width)


def natural(block, rows, width, total):
    _, rem, _ = split(width)
    rems = unfold(block[:TALL_FOLD], rows, total * rem, TALL_FOLD)
    mains = [block[TALL_FOLD + k * rows : TALL_FOLD + (k + 1) * rows] for k in range(total)]
    return [
        jnp.concatenate([main, rems[:, k * rem : (k + 1) * rem]], axis=1)
        for k, main in enumerate(mains)
    ]


def tall_pack(out_ref, values, width):
    main, rem, _ = split(width)
    rows, lanes = values[0].shape[0], rem * len(values)
    for k, value in enumerate(values):
        top = TALL_FOLD + k * rows
        out_ref[0, top : top + rows, :] = value[:, :main].astype(out_ref.dtype)
        for at in range(0, rows, TALL_FOLD):
            deep, left = min(TALL_FOLD, rows - at), at // TALL_FOLD * lanes + k * rem
            part = value[at : at + deep, main:].astype(out_ref.dtype)
            out_ref[0, :deep, left : left + rem] = part


def pack(out_ref, values, width):
    main, rem, lead = split(width)
    for k, value in enumerate(values):
        out_ref[0, lead:, k * main : (k + 1) * main] = value[:, :main].astype(out_ref.dtype)
    rows, lanes = values[0].shape[0], rem * len(values)
    for at in range(0, rows if rem else 0, FOLD):
        deep, left = min(FOLD, rows - at), at // FOLD * lanes
        for k, value in enumerate(values):
            part = value[at : at + deep, main:].astype(out_ref.dtype)
            out_ref[0, :deep, left + k * rem : left + (k + 1) * rem] = part


def mains_and_rems(block, rows, rem, lead, total):
    mains = block[lead:]
    return mains, (unfold(block[:lead], rows, total * rem) if rem else None)


def place(bits, position):
    offset = 0
    for at, weight in bits:
        offset = offset ^ (((position >> at) & 1) * weight)
    return offset


def walk(refs, step, carry):
    base = 0
    for ref in refs:
        count = ref.shape[0]
        if count <= 4:
            for i in range(count):
                carry = step(base + i, ref[i], carry)
        else:
            carry = lax.fori_loop(
                0, count, lambda i, c, ref=ref, base=base: step(base + i, ref[i], c), carry
            )
        base += count
    return carry


def panel_product(left, right, lhs, total, width, rows, places):
    row_bits, depth_bits, col_bits = places
    main, rem, lead = split(width)
    parts, top = width // rows, aligned(rows)
    my_row, my_depth, my_col = (lax.axis_index(a) for a in ("row", "depth", "col"))
    layers = lax.axis_size("depth")

    def fill(position, block, carry):
        col = my_col ^ place(col_bits, position)
        mains, rems = mains_and_rems(block, rows, rem, lead, total)
        for k in range(total):
            whole = mains[:, k * main : (k + 1) * main]
            if rem:
                whole = jnp.concatenate([whole, rems[:, k * rem : (k + 1) * rem]], axis=1)
            for h in range(parts):
                lhs[col * parts + h, k * top : k * top + rows, :] = whole[:, h * rows : (h + 1) * rows]
        return carry

    walk(left, fill, 0)

    def multiply(position, block, carry):
        row = my_row ^ place(row_bits, position)
        depth = my_depth ^ place(depth_bits, position)
        factor = lhs[row * layers + depth]
        operands = mains_and_rems(block, rows, rem, lead, 2)
        return tuple(
            c + jnp.dot(factor, o, preferred_element_type=jnp.float32)
            for c, o in zip(carry, operands[: len(carry)], strict=True)
        )

    sizes = (2 * main, 2 * rem) if rem else (2 * main,)
    zeros = tuple(jnp.zeros((lhs.shape[1], size), jnp.float32) for size in sizes)
    return walk(right, multiply, zeros)


def first_kernel(counts, places, width, *refs):
    n_left, n_right = counts
    left, right = refs[:n_left], refs[n_left : n_left + n_right]
    out_ref, lhs = refs[n_left + n_right :]
    main, rem, lead = split(width)
    rows = out_ref.shape[1] - lead
    top = aligned(rows)
    sums = panel_product(left, right, lhs, 2, width, rows, places)
    results = []
    for acc in sums:
        size = acc.shape[1] // 2
        square = acc[:rows, :size]
        cross = acc[top : top + rows, :size] + acc[:rows, size:]
        high = cross.astype(jnp.bfloat16).astype(jnp.float32)
        results.append((high, cross - high, square))
    for k, value in enumerate(results[0]):
        out_ref[0, lead:, k * main : (k + 1) * main] = value.astype(out_ref.dtype)
    if rem:
        folded = fold(jnp.concatenate(results[1], axis=1))
        out_ref[0, :FOLD, : folded.shape[1]] = folded.astype(out_ref.dtype)


def last_kernel(counts, places, width, *refs):
    n_left, n_right = counts
    left, right = refs[:n_left], refs[n_left : n_left + n_right]
    own_ref, out_ref, lhs = refs[n_left + n_right :]
    main, rem, lead = split(width)
    rows = out_ref.shape[0]
    top = aligned(rows)
    sums = panel_product(left, right, lhs, 3, width, rows, places)
    owns = mains_and_rems(own_ref[0], rows, rem, lead, 2)
    for acc, own, base in zip(sums, owns, (0, main)):
        size = acc.shape[1] // 2
        total = acc[:rows, :size] + acc[top : top + rows, :size] + acc[2 * top : 2 * top + rows, size:]
        out_ref[:, base : base + size] = 1.5 * own[:, size:].astype(jnp.float32) - 0.5 * total


def times(left, right):
    return jnp.dot(left, right, preferred_element_type=jnp.float32)


def add_panels(offsets, mine, others, lhs, rhs, width, rows):
    my_row, my_depth = lax.axis_index("row"), lax.axis_index("depth")
    top = aligned(rows)
    square = cross = jnp.zeros((rows, width), jnp.float32)
    for k, offset in enumerate(offsets):
        row = lax.rem(my_row + offset, lax.axis_size("row"))
        panels = []
        for a, b in zip(
            natural(mine[k], rows, width, 2), natural(others[k], rows, width, 2), strict=True
        ):
            halves = [jnp.where(my_depth == 0, a, b), jnp.where(my_depth == 0, b, a)]
            halves = [half.astype(jnp.float32) for half in halves]
            panels.append(jnp.concatenate(halves, axis=0).astype(jnp.bfloat16))
        for which, panel in enumerate(panels):
            rhs[row, which] = panel
        both = times(lhs[row], panels[0])
        square += both[:rows]
        cross += both[top : top + rows] + times(lhs[row, :rows], panels[1])
    return square, cross


def firsts_kernel(offsets, width, own, beside, *refs):
    mine, others = refs[: len(offsets)], refs[len(offsets) : 2 * len(offsets)]
    out_ref, low_ref, rhs, lhs = refs[2 * len(offsets) :]
    rows = (own.shape[1] - TALL_FOLD) // 2
    top = aligned(rows)
    my_col = lax.axis_index("col")
    for ref, across in ((own, 0), (beside, 1)):
        for k in range(2):
            col = my_col ^ across ^ (3 * k)
            for which, part in enumerate(natural(ref[k], rows, width, 2)):
                lhs[col, which * top : which * top + rows, :] = part
    square = cross = jnp.zeros((rows, width), jnp.float32)
    for row_offsets, left, right in zip(offsets, mine, others, strict=True):
        terms = add_panels(row_offsets, left, right, lhs, rhs, width, rows)
        square, cross = square + terms[0], cross + terms[1]
    high = cross.astype(jnp.bfloat16).astype(jnp.float32)
    tall_pack(out_ref, (high, square), width)
    low = (cross - high).astype(low_ref.dtype)
    low_ref[...] = jnp.zeros_like(low_ref)
    low_ref[0, TALL_FOLD : TALL_FOLD + rows, :] = low[:, :LANES]
    low_ref[0, TALL_FOLD + rows :, : width - LANES] = low[:, LANES:]


def panel_terms(col, block, low, rhs, width, rows):
    main, rem, _ = split(width)
    first, second = TALL_FOLD, TALL_FOLD + rows
    total = times(block[first:second], rhs[col, 0, :main])
    total += times(block[second:], rhs[col, 1, :main])
    ends = jnp.concatenate([rhs[col, 0, main:], rhs[col, 1, main:]], axis=0)
    total += times(unfold(block[:first], rows, 2 * rem, TALL_FOLD), ends)
    if low is not None:
        total += times(low[first:second], rhs[col, 0, :main])
        total += times(low[second:, :rem], rhs[col, 0, main:])
    return total


def far_lasts_kernel(offset, width, panel, rhs, own_ref, out_ref):
    rows = out_ref.shape[0]
    terms = panel_terms(lax.axis_index("col") ^ offset, panel[0], None, rhs, width, rows)
    own = natural(own_ref[0], rows, width, 2)[1].astype(jnp.float32)
    out_ref[...] = 1.5 * own - 0.5 * terms


def near_lasts_kernel(width, mine, other, rhs, early, out_ref, ends_ref):
    rows = out_ref.shape[0]
    my_col = lax.axis_index("col")
    terms = panel_terms(my_col, mine[0], mine[1], rhs, width, rows)
    terms += panel_terms(my_col ^ 1, other[0], other[1], rhs, width, rows)
    out_ref[...] = early[...] - 0.5 * terms
    main, rem, _ = split(width)
    col = my_col ^ 2
    ends_ref[...] = jnp.zeros_like(ends_ref)
    for group in range(ends_ref.shape[0]):
        for which in range(2):
            at = (2 * group + which) * rem
            ends_ref[group, at : at + rem] = rhs[col, which, main:]


def late_lasts_kernel(offset, width, panel, rhs, early, ends, out_ref):
    rows, main = out_ref.shape[0], split(width)[0]
    col = lax.axis_index("col") ^ offset
    first, second = TALL_FOLD, TALL_FOLD + rows
    terms = times(panel[0, first:second], rhs[col, 0, :main])
    terms += times(panel[0, second:], rhs[col, 1, :main])
    folded = panel[0, :first, : ends.shape[1]]
    groups = [times(folded, ends[group]) for group in range(ends.shape[0])]
    out_ref[...] = early[...] - 0.5 * (terms + jnp.concatenate(groups, axis=0))


def call(kernel, name, out_shape, operands, scratch=(), **kwargs):
    return pl.pallas_call(
        kernel,
        out_shape=out_shape,
        in_specs=[VMEM] * len(operands),
        out_specs=jax.tree.map(lambda _: VMEM, out_shape),
        scratch_shapes=list(scratch),
        compiler_params=PARAMS,
        name=name,
        **kwargs,
    )(*operands)


def fast_body(block, rows, width):
    grid, top = lax.axis_size("row"), aligned(rows)
    shape = jax.ShapeDtypeStruct
    opposite = turn(block, "row", 2)
    line = jnp.concatenate([turn(block, "row", 1), turn(block, "row", 3), block], axis=0)
    side_line = swap(line, "depth", 1)
    side_opposite = swap(opposite, "depth", 1)
    held = jnp.concatenate([block, swap(block, "col", 3)], axis=0)
    beside = swap(held, "col", 1)
    panels = shape((grid, 2, width, width), jnp.bfloat16)
    firsts, low, rhs = call(
        functools.partial(firsts_kernel, ((1, 3, 0), (2,)), width),
        "firsts",
        (shape(block.shape, block.dtype), shape(block.shape, block.dtype), panels),
        (held, beside, line, opposite, side_line, side_opposite),
        [pltpu.VMEM((grid, 2 * top, width), jnp.bfloat16)],
    )
    out = shape((rows, width), jnp.float32)
    straight = swap(firsts, "col", 3)
    crossed = swap(firsts, "col", 2)
    mine = jnp.concatenate([firsts, low], axis=0)
    near = (mine, swap(mine, "col", 1))
    far = call(functools.partial(far_lasts_kernel, 3, width), "far_lasts", out, (straight, rhs, block), cost_estimate=pl.CostEstimate(flops=1000000000, bytes_accessed=0, transcendentals=0),)
    rem, groups = split(width)[1], rows // TALL_FOLD
    ends = shape((groups, groups * 2 * rem, width), block.dtype)
    total, ends = call(
        functools.partial(near_lasts_kernel, width), "near_lasts", (out, ends), (*near, rhs, far)
    )
    return call(
        functools.partial(late_lasts_kernel, 2, width), "late_lasts", out, (crossed, rhs, total, ends)
    )


def gather(block, axes):
    held, at, bits = block, 0, []
    for axis, steps in axes:
        meaning = []
        for step in steps:
            held = jnp.concatenate([held, swap(held, axis, step)], axis=0)
            meaning.append((at, step))
            at += 1
        bits.append(meaning)
    return [held], bits


def general_body(block, rows, width):
    def steps(axis):
        return [1 << k for k in range(lax.axis_size(axis).bit_length() - 1)]

    right, (row_bits, depth_bits) = gather(block, [(a, steps(a)) for a in ("row", "depth")])
    left, (col_bits,) = gather(block, [("col", steps("col")[::-1])])
    places = (row_bits, depth_bits, col_bits)
    blocks, top = right[0].shape[0], aligned(rows)
    _, _, lead = split(width)
    firsts = call(
        functools.partial(first_kernel, (1, 1), places, width),
        "firsts",
        jax.ShapeDtypeStruct((1, lead + rows, 3 * split(width)[0]), jnp.bfloat16),
        (*left, *right),
        [pltpu.VMEM((blocks, 2 * top, rows), jnp.bfloat16)],
    )
    left, (col_bits,) = gather(firsts, [("col", steps("col")[::-1])])
    return call(
        functools.partial(last_kernel, (1, 1), places, width),
        "lasts",
        jax.ShapeDtypeStruct((rows, width), jnp.float32),
        (*left, *right, block),
        [pltpu.VMEM((blocks, 3 * top, rows), jnp.bfloat16)],
    )


def body(x_matrix, tangent, fill_x, fill_t):
    rows, width = x_matrix.shape
    sizes = tuple(lax.axis_size(a) for a in ("row", "col", "depth"))
    main, rem, lead = split(width)
    fast = sizes == (4, 4, 2) and main == LANES and rem > 0 and rows % TALL_FOLD == 0
    fast = fast and 2 * rem * (rows // TALL_FOLD) <= LANES
    packed = (TALL_FOLD + 2 * rows, LANES) if fast else (lead + rows, 2 * main)
    block = pl.pallas_call(
        functools.partial(pack_kernel, tall_pack if fast else pack),
        out_shape=jax.ShapeDtypeStruct((1, *packed), jnp.bfloat16),
        in_specs=[HBM] * 4,
        out_specs=VMEM,
        scratch_shapes=[
            pltpu.VMEM((rows, width), jnp.bfloat16),
            pltpu.VMEM((rows, width), jnp.bfloat16),
            pltpu.SMEM(fill_x.shape, jnp.int32),
            pltpu.SMEM(fill_t.shape, jnp.int32),
            pltpu.SemaphoreType.DMA((4,)),
        ],
        compiler_params=PARAMS,
        name="pack",
    )(*(pltpu.with_memory_space_constraint(a, pltpu.HBM) for a in (x_matrix, tangent, fill_x, fill_t)))
    return (fast_body if fast else general_body)(block, rows, width)


def solution(mesh):
    placed = (P(("row", "depth"), "col"), P(("row", "depth"), "col"), P(), P())
    return jax.shard_map(
        body, mesh=mesh, in_specs=placed, out_specs=P(("row", "depth"), "col"), check_vma=False
    )
```

```python
import functools

import jax
import jax.numpy as jnp
from jax import lax
from jax.experimental import pallas as pl
from jax.experimental.pallas import tpu as pltpu
from jax.sharding import PartitionSpec as P

BLOCK = 128
LANES = 128
FOLD = 16
TALL_FOLD = 24
HBM = pl.BlockSpec(memory_space=pltpu.HBM)
VMEM = pl.BlockSpec(memory_space=pltpu.VMEM)
PARAMS = pltpu.CompilerParams(vmem_limit_bytes=48 * 1024 * 1024)


def aligned(rows):
    return -(-rows // 16) * 16


def split(width):
    rem = width % LANES
    return width - rem, rem, FOLD if rem else 0


def swap(value, axis, offset):
    size = lax.axis_size(axis)
    return lax.ppermute(value, axis, [(i, i ^ offset) for i in range(size)])


def turn(value, axis, offset):
    size = lax.axis_size(axis)
    return lax.ppermute(value, axis, [((i + offset) % size, i) for i in range(size)])


def block_fill(fill_ref, row_start, col_start, rows, width):
    count = fill_ref.shape[0]
    row_ids = row_start + lax.broadcasted_iota(jnp.int32, (rows, width), 0)
    col_ids = col_start + lax.broadcasted_iota(jnp.int32, (1, width), 1)
    first_row, first_col = row_start // BLOCK, col_start // BLOCK
    mask = None
    for i in range((rows - 2) // BLOCK + 2):
        row_at = jnp.minimum(first_row + i, count - 1)
        flags = None
        for j in range((width - 2) // BLOCK + 2):
            flag = fill_ref[row_at, jnp.minimum(first_col + j, count - 1)].astype(jnp.float32)
            passed = col_ids >= (first_col + j) * BLOCK
            flags = jnp.where(passed, flag, 0.0 if flags is None else flags)
        flags = jnp.broadcast_to(flags, (rows, width))
        mask = flags if mask is None else jnp.where(row_ids >= (first_row + i) * BLOCK, flags, mask)
    return mask


def fold(value):
    rows, lanes = value.shape
    spare = -rows % FOLD
    if spare:
        value = jnp.concatenate([value, jnp.zeros((spare, lanes), value.dtype)], axis=0)
    return jnp.concatenate([value[at : at + FOLD] for at in range(0, rows, FOLD)], axis=1)


def unfold(value, rows, lanes, deep=FOLD):
    groups = [value[:, k * lanes : (k + 1) * lanes] for k in range(-(-rows // deep))]
    return jnp.concatenate(groups, axis=0)[:rows]


def pack_kernel(
    packer, x_hbm, t_hbm, fill_x_hbm, fill_t_hbm, out_ref, x_ref, t_ref, fill_x_ref, fill_t_ref, sems
):
    rows, width = x_ref.shape
    pairs = ((fill_x_hbm, fill_x_ref), (fill_t_hbm, fill_t_ref), (x_hbm, x_ref), (t_hbm, t_ref))
    copies = [pltpu.make_async_copy(src, dst, sems.at[k]) for k, (src, dst) in enumerate(pairs)]
    for copy in copies:
        copy.start()
    row_at = lax.axis_index("row") * lax.axis_size("depth") + lax.axis_index("depth")
    row_start, col_start = row_at * rows, lax.axis_index("col") * width
    copies[0].wait()
    copies[1].wait()
    masks = [block_fill(ref, row_start, col_start, rows, width) for ref in (fill_x_ref, fill_t_ref)]
    copies[2].wait()
    copies[3].wait()
    masked = [x_ref[...].astype(jnp.float32) * masks[0], t_ref[...].astype(jnp.float32) * masks[1]]
    packer(out_ref, masked, width)


def natural(block, rows, width, total):
    _, rem, _ = split(width)
    rems = unfold(block[:TALL_FOLD], rows, total * rem, TALL_FOLD)
    mains = [block[TALL_FOLD + k * rows : TALL_FOLD + (k + 1) * rows] for k in range(total)]
    return [
        jnp.concatenate([main, rems[:, k * rem : (k + 1) * rem]], axis=1)
        for k, main in enumerate(mains)
    ]


def tall_pack(out_ref, values, width):
    main, rem, _ = split(width)
    rows, lanes = values[0].shape[0], rem * len(values)
    for k, value in enumerate(values):
        top = TALL_FOLD + k * rows
        out_ref[0, top : top + rows, :] = value[:, :main].astype(out_ref.dtype)
        for at in range(0, rows, TALL_FOLD):
            deep, left = min(TALL_FOLD, rows - at), at // TALL_FOLD * lanes + k * rem
            part = value[at : at + deep, main:].astype(out_ref.dtype)
            out_ref[0, :deep, left : left + rem] = part


def pack(out_ref, values, width):
    main, rem, lead = split(width)
    for k, value in enumerate(values):
        out_ref[0, lead:, k * main : (k + 1) * main] = value[:, :main].astype(out_ref.dtype)
    rows, lanes = values[0].shape[0], rem * len(values)
    for at in range(0, rows if rem else 0, FOLD):
        deep, left = min(FOLD, rows - at), at // FOLD * lanes
        for k, value in enumerate(values):
            part = value[at : at + deep, main:].astype(out_ref.dtype)
            out_ref[0, :deep, left + k * rem : left + (k + 1) * rem] = part


def mains_and_rems(block, rows, rem, lead, total):
    mains = block[lead:]
    return mains, (unfold(block[:lead], rows, total * rem) if rem else None)


def place(bits, position):
    offset = 0
    for at, weight in bits:
        offset = offset ^ (((position >> at) & 1) * weight)
    return offset


def walk(refs, step, carry):
    base = 0
    for ref in refs:
        count = ref.shape[0]
        if count <= 4:
            for i in range(count):
                carry = step(base + i, ref[i], carry)
        else:
            carry = lax.fori_loop(
                0, count, lambda i, c, ref=ref, base=base: step(base + i, ref[i], c), carry
            )
        base += count
    return carry


def panel_product(left, right, lhs, total, width, rows, places):
    row_bits, depth_bits, col_bits = places
    main, rem, lead = split(width)
    parts, top = width // rows, aligned(rows)
    my_row, my_depth, my_col = (lax.axis_index(a) for a in ("row", "depth", "col"))
    layers = lax.axis_size("depth")

    def fill(position, block, carry):
        col = my_col ^ place(col_bits, position)
        mains, rems = mains_and_rems(block, rows, rem, lead, total)
        for k in range(total):
            whole = mains[:, k * main : (k + 1) * main]
            if rem:
                whole = jnp.concatenate([whole, rems[:, k * rem : (k + 1) * rem]], axis=1)
            for h in range(parts):
                lhs[col * parts + h, k * top : k * top + rows, :] = whole[:, h * rows : (h + 1) * rows]
        return carry

    walk(left, fill, 0)

    def multiply(position, block, carry):
        row = my_row ^ place(row_bits, position)
        depth = my_depth ^ place(depth_bits, position)
        factor = lhs[row * layers + depth]
        operands = mains_and_rems(block, rows, rem, lead, 2)
        return tuple(
            c + jnp.dot(factor, o, preferred_element_type=jnp.float32)
            for c, o in zip(carry, operands[: len(carry)], strict=True)
        )

    sizes = (2 * main, 2 * rem) if rem else (2 * main,)
    zeros = tuple(jnp.zeros((lhs.shape[1], size), jnp.float32) for size in sizes)
    return walk(right, multiply, zeros)


def first_kernel(counts, places, width, *refs):
    n_left, n_right = counts
    left, right = refs[:n_left], refs[n_left : n_left + n_right]
    out_ref, lhs = refs[n_left + n_right :]
    main, rem, lead = split(width)
    rows = out_ref.shape[1] - lead
    top = aligned(rows)
    sums = panel_product(left, right, lhs, 2, width, rows, places)
    results = []
    for acc in sums:
        size = acc.shape[1] // 2
        square = acc[:rows, :size]
        cross = acc[top : top + rows, :size] + acc[:rows, size:]
        high = cross.astype(jnp.bfloat16).astype(jnp.float32)
        results.append((high, cross - high, square))
    for k, value in enumerate(results[0]):
        out_ref[0, lead:, k * main : (k + 1) * main] = value.astype(out_ref.dtype)
    if rem:
        folded = fold(jnp.concatenate(results[1], axis=1))
        out_ref[0, :FOLD, : folded.shape[1]] = folded.astype(out_ref.dtype)


def last_kernel(counts, places, width, *refs):
    n_left, n_right = counts
    left, right = refs[:n_left], refs[n_left : n_left + n_right]
    own_ref, out_ref, lhs = refs[n_left + n_right :]
    main, rem, lead = split(width)
    rows = out_ref.shape[0]
    top = aligned(rows)
    sums = panel_product(left, right, lhs, 3, width, rows, places)
    owns = mains_and_rems(own_ref[0], rows, rem, lead, 2)
    for acc, own, base in zip(sums, owns, (0, main)):
        size = acc.shape[1] // 2
        total = acc[:rows, :size] + acc[top : top + rows, :size] + acc[2 * top : 2 * top + rows, size:]
        out_ref[:, base : base + size] = 1.5 * own[:, size:].astype(jnp.float32) - 0.5 * total


def times(left, right):
    return jnp.dot(left, right, preferred_element_type=jnp.float32)


def add_panels(offsets, mine, others, lhs, rhs, width, rows):
    my_row, my_depth = lax.axis_index("row"), lax.axis_index("depth")
    top = aligned(rows)
    square = cross = jnp.zeros((rows, width), jnp.float32)
    for k, offset in enumerate(offsets):
        row = lax.rem(my_row + offset, lax.axis_size("row"))
        panels = []
        for a, b in zip(
            natural(mine[k], rows, width, 2), natural(others[k], rows, width, 2), strict=True
        ):
            halves = [jnp.where(my_depth == 0, a, b), jnp.where(my_depth == 0, b, a)]
            panels.append(jnp.concatenate(halves, axis=0))
        for which, panel in enumerate(panels):
            rhs[row, which] = panel
        both = times(lhs[row], panels[0])
        square += both[:rows]
        cross += both[top : top + rows] + times(lhs[row, :rows], panels[1])
    return square, cross


def firsts_kernel(offsets, width, own, beside, *refs):
    mine, others = refs[: len(offsets)], refs[len(offsets) : 2 * len(offsets)]
    out_ref, low_ref, rhs, lhs = refs[2 * len(offsets) :]
    rows = (own.shape[1] - TALL_FOLD) // 2
    top = aligned(rows)
    my_col = lax.axis_index("col")
    for ref, across in ((own, 0), (beside, 1)):
        for k in range(2):
            col = my_col ^ across ^ (3 * k)
            for which, part in enumerate(natural(ref[k], rows, width, 2)):
                lhs[col, which * top : which * top + rows, :] = part
    square = cross = jnp.zeros((rows, width), jnp.float32)
    for row_offsets, left, right in zip(offsets, mine, others, strict=True):
        terms = add_panels(row_offsets, left, right, lhs, rhs, width, rows)
        square, cross = square + terms[0], cross + terms[1]
    high = cross.astype(jnp.bfloat16).astype(jnp.float32)
    tall_pack(out_ref, (high, square), width)
    low = (cross - high).astype(low_ref.dtype)
    low_ref[...] = jnp.zeros_like(low_ref)
    low_ref[0, TALL_FOLD : TALL_FOLD + rows, :] = low[:, :LANES]
    low_ref[0, TALL_FOLD + rows :, : width - LANES] = low[:, LANES:]


def panel_terms(col, block, low, rhs, width, rows):
    main, rem, _ = split(width)
    first, second = TALL_FOLD, TALL_FOLD + rows
    total = times(block[first:second], rhs[col, 0, :main])
    total += times(block[second:], rhs[col, 1, :main])
    ends = jnp.concatenate([rhs[col, 0, main:], rhs[col, 1, main:]], axis=0)
    total += times(unfold(block[:first], rows, 2 * rem, TALL_FOLD), ends)
    if low is not None:
        total += times(low[first:second], rhs[col, 0, :main])
        total += times(low[second:, :rem], rhs[col, 0, main:])
    return total


def far_lasts_kernel(offset, width, panel, rhs, own_ref, out_ref):
    rows = out_ref.shape[0]
    terms = panel_terms(lax.axis_index("col") ^ offset, panel[0], None, rhs, width, rows)
    own = natural(own_ref[0], rows, width, 2)[1].astype(jnp.float32)
    out_ref[...] = 1.5 * own - 0.5 * terms


def near_lasts_kernel(width, mine, other, rhs, early, out_ref, ends_ref):
    rows = out_ref.shape[0]
    my_col = lax.axis_index("col")
    terms = panel_terms(my_col, mine[0], mine[1], rhs, width, rows)
    terms += panel_terms(my_col ^ 1, other[0], other[1], rhs, width, rows)
    out_ref[...] = early[...] - 0.5 * terms
    main, rem, _ = split(width)
    col = my_col ^ 2
    ends_ref[...] = jnp.zeros_like(ends_ref)
    for group in range(ends_ref.shape[0]):
        for which in range(2):
            at = (2 * group + which) * rem
            ends_ref[group, at : at + rem] = rhs[col, which, main:]


def late_lasts_kernel(offset, width, panel, rhs, early, ends, out_ref):
    rows, main = out_ref.shape[0], split(width)[0]
    col = lax.axis_index("col") ^ offset
    first, second = TALL_FOLD, TALL_FOLD + rows
    terms = times(panel[0, first:second], rhs[col, 0, :main])
    terms += times(panel[0, second:], rhs[col, 1, :main])
    folded = panel[0, :first, : ends.shape[1]]
    groups = [times(folded, ends[group]) for group in range(ends.shape[0])]
    out_ref[...] = early[...] - 0.5 * (terms + jnp.concatenate(groups, axis=0))


def call(kernel, name, out_shape, operands, scratch=(), **kwargs):
    return pl.pallas_call(
        kernel,
        out_shape=out_shape,
        in_specs=[VMEM] * len(operands),
        out_specs=jax.tree.map(lambda _: VMEM, out_shape),
        scratch_shapes=list(scratch),
        compiler_params=PARAMS,
        name=name,
        **kwargs,
    )(*operands)


def fast_body(block, rows, width):
    grid, top = lax.axis_size("row"), aligned(rows)
    shape = jax.ShapeDtypeStruct
    opposite = turn(block, "row", 2)
    line = jnp.concatenate([turn(block, "row", 1), turn(block, "row", 3), block], axis=0)
    side_line = swap(line, "depth", 1)
    side_opposite = swap(opposite, "depth", 1)
    held = jnp.concatenate([block, swap(block, "col", 3)], axis=0)
    beside = swap(held, "col", 1)
    panels = shape((grid, 2, width, width), jnp.bfloat16)
    firsts, low, rhs = call(
        functools.partial(firsts_kernel, ((1, 3, 0), (2,)), width),
        "firsts",
        (shape(block.shape, block.dtype), shape(block.shape, block.dtype), panels),
        (held, beside, line, opposite, side_line, side_opposite),
        [pltpu.VMEM((grid, 2 * top, width), jnp.bfloat16)],
    )
    out = shape((rows, width), jnp.float32)
    straight = swap(firsts, "col", 3)
    crossed = swap(firsts, "col", 2)
    mine = jnp.concatenate([firsts, low], axis=0)
    near = (mine, swap(mine, "col", 1))
    far = call(functools.partial(far_lasts_kernel, 3, width), "far_lasts", out, (straight, rhs, block), cost_estimate=pl.CostEstimate(flops=1000000000, bytes_accessed=0, transcendentals=0),)
    rem, groups = split(width)[1], rows // TALL_FOLD
    ends = shape((groups, groups * 2 * rem, width), block.dtype)
    total, ends = call(
        functools.partial(near_lasts_kernel, width), "near_lasts", (out, ends), (*near, rhs, far)
    )
    return call(
        functools.partial(late_lasts_kernel, 2, width), "late_lasts", out, (crossed, rhs, total, ends)
    )


def gather(block, axes):
    held, at, bits = block, 0, []
    for axis, steps in axes:
        meaning = []
        for step in steps:
            held = jnp.concatenate([held, swap(held, axis, step)], axis=0)
            meaning.append((at, step))
            at += 1
        bits.append(meaning)
    return [held], bits


def general_body(block, rows, width):
    def steps(axis):
        return [1 << k for k in range(lax.axis_size(axis).bit_length() - 1)]

    right, (row_bits, depth_bits) = gather(block, [(a, steps(a)) for a in ("row", "depth")])
    left, (col_bits,) = gather(block, [("col", steps("col")[::-1])])
    places = (row_bits, depth_bits, col_bits)
    blocks, top = right[0].shape[0], aligned(rows)
    _, _, lead = split(width)
    firsts = call(
        functools.partial(first_kernel, (1, 1), places, width),
        "firsts",
        jax.ShapeDtypeStruct((1, lead + rows, 3 * split(width)[0]), jnp.bfloat16),
        (*left, *right),
        [pltpu.VMEM((blocks, 2 * top, rows), jnp.bfloat16)],
    )
    left, (col_bits,) = gather(firsts, [("col", steps("col")[::-1])])
    return call(
        functools.partial(last_kernel, (1, 1), places, width),
        "lasts",
        jax.ShapeDtypeStruct((rows, width), jnp.float32),
        (*left, *right, block),
        [pltpu.VMEM((blocks, 3 * top, rows), jnp.bfloat16)],
    )


def body(x_matrix, tangent, fill_x, fill_t):
    rows, width = x_matrix.shape
    sizes = tuple(lax.axis_size(a) for a in ("row", "col", "depth"))
    main, rem, lead = split(width)
    fast = sizes == (4, 4, 2) and main == LANES and rem > 0 and rows % TALL_FOLD == 0
    fast = fast and 2 * rem * (rows // TALL_FOLD) <= LANES
    packed = (TALL_FOLD + 2 * rows, LANES) if fast else (lead + rows, 2 * main)
    block = pl.pallas_call(
        functools.partial(pack_kernel, tall_pack if fast else pack),
        out_shape=jax.ShapeDtypeStruct((1, *packed), jnp.bfloat16),
        in_specs=[HBM] * 4,
        out_specs=VMEM,
        scratch_shapes=[
            pltpu.VMEM((rows, width), jnp.bfloat16),
            pltpu.VMEM((rows, width), jnp.bfloat16),
            pltpu.SMEM(fill_x.shape, jnp.int32),
            pltpu.SMEM(fill_t.shape, jnp.int32),
            pltpu.SemaphoreType.DMA((4,)),
        ],
        compiler_params=PARAMS,
        name="pack",
    )(*(pltpu.with_memory_space_constraint(a, pltpu.HBM) for a in (x_matrix, tangent, fill_x, fill_t)))
    return (fast_body if fast else general_body)(block, rows, width)


def solution(mesh):
    placed = (P(("row", "depth"), "col"), P(("row", "depth"), "col"), P(), P())
    return jax.shard_map(
        body, mesh=mesh, in_specs=placed, out_specs=P(("row", "depth"), "col"), check_vma=False
    )
```
